128 devices in a mesh: outer: 8 (over x, core), inner: 16 (over z, y).
Axes of the slice: x: 4, y: 4, z: 4, core: 2. Of those that a mesh axis runs over, the one named last changes fastest.
Arguments:
- grad_out: bfloat16 [16384, 4096], P(('outer', 'inner')), may hold values from -6 to 6
- route_weights: bfloat16 [16384, 8], P(('outer', 'inner')), may hold values from 0.049804688 to 1
- routes: int32 [16384, 8], P(('outer', 'inner')), may hold values from 0 to 15, all different within a row; in each aligned block of 128 rows (0 to 127, 128 to 255, ...) at most 96 rows name the same one
- saved_gate_up: bfloat16 [8, 16, 16, 96, 3072], P(None, 'outer', 'inner'), may hold values from -6 to 6
- down_weight: bfloat16 [16, 1536, 4096], P('outer', None, 'inner'), may hold values from -0.09375 to 0.09375
Outputs:
- grad_gate_up: bfloat16 [8, 16, 16, 96, 3072], P(None, 'outer', 'inner')
- grad_weights: float32 [16384, 8], P(('outer', 'inner'))
The draws below stay inside these ranges and needn't reach their ends.
Inputs may be any that keep to these rules, and one draw needn't show every extreme that they name: `routes`: each row names 8 different experts. In each aligned block of 128 rows (the rows of one device) no expert is named more than 96 times, a bound that some block reaches.
All inputs are finite; a program needn't handle non-finite values.
Results may differ from the reference program's by a relative error of at most 0.0029.
Values may be sent and summed in bfloat16 or wider, within the bound.
No kernel may reach another device: no remote copies, remote signals or barrier semaphores. Data moves between devices by JAX's collectives and lax.ppermute only.
A program may use at most 192 MiB of HBM per device.

```python
import math
import jax
import jax.numpy as jnp
import numpy as np
from jax import lax

D = 4096
HID = 1536
TOP = 8
TOK_DEV = 128
EXPERTS = 16
CAP = 96
TOKENS = 16384
N_OUTER = 8
N_INNER = 16


def block_scale(own_key, extent, shards, least, high):
    def one(dim, blocks):
        draws = jax.random.uniform(jax.random.fold_in(jax.random.fold_in(own_key, 6), dim), (blocks,), jnp.float32, least / len(shards), high / len(shards))
        return jnp.repeat(jnp.exp(draws), extent[dim] // blocks).reshape((-1,) + (1,) * (len(extent) - dim - 1))

    level = one(*shards[0])
    for cut in shards[1:]:
        level = level * one(*cut)
    return level


def shared_out(key, own, number, rows, amount, top, most, slope):
    sequence = jax.random.permutation(key, amount)
    packed, usual = load_shares(amount, rows * top, most, slope, True), load_shares(amount, rows * top, most, slope, False)
    places = jnp.arange(amount)

    def named(lengths, offset_by):
        used = int((lengths > 0).sum())
        fixed = max(1, used // 4)
        moved = fixed + (places - fixed + offset_by * (used - fixed)) % max(1, amount - fixed)
        return jnp.zeros((amount,), jnp.int32).at[sequence[jnp.where(places < fixed, places, moved)]].set(jnp.asarray(lengths, jnp.int32))

    lengths = jnp.where(number % 4 == 0, named(packed, number // 4), named(usual, number - number // 4 - 1))
    mixed = jax.random.permutation(jax.random.fold_in(own, 3), amount)
    source_of, receiver = mixed[0:amount // 2 * 2:2], mixed[1:amount // 2 * 2:2]
    room = jnp.minimum(lengths[source_of] - 1, most - lengths[receiver]) // 2
    room = jnp.where((source_of == sequence[0]) | (receiver == sequence[0]) | (lengths[receiver] == 0), 0, jnp.maximum(room, 0))
    moved = jax.random.randint(jax.random.fold_in(own, 4), (amount // 2,), 0, 1 << 20) % (room + 1)
    lengths = lengths.at[source_of].add(-moved).at[receiver].add(moved)
    members = jnp.searchsorted(jnp.cumsum(lengths), jnp.arange(rows * top), side="right").astype(jnp.int32)
    table = members.reshape(top, rows).T
    table = table[jax.random.permutation(jax.random.fold_in(own, 1), rows)]
    offset_by = jax.random.randint(jax.random.fold_in(own, 2), (rows, 1), 0, top)
    return jnp.take_along_axis(table, (jnp.arange(top)[None, :] + offset_by) % top, axis=1)


def load_shares(count, total, reach, lean, full):
    weights = [(1 << 20) // math.isqrt(rank ** lean) + 1 for rank in range(1, count + 1)]
    largest = reach if full else min(reach, max(-(-total // count), total * weights[0] // sum(weights)))
    least = 1 if total - largest >= count - 1 else 0
    counts, spare = [largest] + [least] * (count - 1), total - largest - least * (count - 1)
    while spare > 0:
        movable = [i for i in range(1, count) if counts[i] < largest] or [i for i in range(1, count) if counts[i] < reach]
        pool, left = sum([weights[i] for i in movable]), spare
        for i in movable:
            more = min(reach - counts[i], max(1, left * weights[i] // pool), spare)
            counts[i] = counts[i] + more
            spare = spare - more
    return np.array(counts)


def normal_values(key, dims, spread, most, shards=(), kind=jnp.bfloat16):
    drawn = spread * jax.random.normal(key, dims, jnp.float32)
    if shards:
        drawn = drawn * block_scale(key, dims, shards, -0.22, 0.18)
    return jnp.clip(drawn, -most, most).astype(kind)


def setup_inputs(seed: int = 0) -> dict:
    arg_keys = jax.random.split(jax.random.key(seed), 6)
    grad_out = normal_values(arg_keys[0], (TOKENS, D), 1.0, 6.0, ((0, 128),))
    route_weights = jnp.clip(jnp.exp(math.log(1.0) - 2.9996462 * jax.random.uniform(arg_keys[1], (TOKENS, TOP), jnp.float32) ** block_scale(arg_keys[1], (TOKENS, TOP), ((0, 128),), -0.2, 0.2)), 0.049804688, 1.0).astype(jnp.bfloat16)
    routes_keys = jax.random.split(jax.random.fold_in(arg_keys[2], 1), TOKENS // TOK_DEV)
    routes_turns = jax.random.permutation(jax.random.fold_in(arg_keys[2], 3), TOKENS // TOK_DEV)
    routes = jax.vmap(lambda own, number: shared_out(jax.random.fold_in(arg_keys[2], 2), own, number, TOK_DEV, EXPERTS, TOP, CAP, 2))(routes_keys, routes_turns).reshape((TOKENS, TOP))
    saved_gate_up = normal_values(arg_keys[3], (N_OUTER, EXPERTS, N_INNER, CAP, 2 * HID), 1.0, 6.0, ((1, 8), (2, 16)))
    down_weight = normal_values(arg_keys[4], (EXPERTS, HID, D), D ** -0.5, 0.09375, ((0, 8), (2, 16)))
    return {"grad_out": grad_out, "route_weights": route_weights, "routes": routes, "saved_gate_up": saved_gate_up, "down_weight": down_weight}


def reference(grad_out, route_weights, routes, saved_gate_up, down_weight):
    blocks = N_OUTER * N_INNER
    pairs = TOK_DEV * TOP
    block_routes = routes.reshape(blocks, pairs)
    onehot = (block_routes[:, :, None] == jnp.arange(EXPERTS, dtype=jnp.int32)[None, None, :]).astype(jnp.int32)
    before = jnp.cumsum(onehot, axis=1) - onehot
    position = jnp.sum(before * onehot, axis=2).astype(jnp.int32)
    slot = (block_routes * CAP + position).astype(jnp.int32)
    pair_index = jnp.arange(blocks * pairs, dtype=jnp.int32).reshape(blocks, pairs)
    owner = jnp.full((blocks, EXPERTS * CAP), -1, jnp.int32)
    owner = owner.at[jnp.arange(blocks, dtype=jnp.int32)[:, None], slot].set(pair_index)
    owner = owner.reshape(N_OUTER, N_INNER, EXPERTS, CAP)
    flat_weights = route_weights.reshape(-1)

    def per_expert(expert):
        index = owner[:, :, expert]
        valid = index >= 0
        safe = jnp.maximum(index, 0)
        rows = jnp.where(valid[..., None], grad_out[safe // TOP], jnp.zeros((), jnp.bfloat16))
        weight = jnp.where(valid, flat_weights[safe], jnp.zeros((), jnp.bfloat16)).astype(jnp.float32)
        matrix = down_weight[expert].astype(jnp.float32)
        carried = jnp.einsum("oicd,hd->oich", rows.astype(jnp.float32), matrix)
        saved = saved_gate_up[:, expert].astype(jnp.float32)
        gate = saved[..., :HID]
        upper = saved[..., HID:]
        sigma = jax.nn.sigmoid(gate)
        active = gate * sigma
        hidden = lax.optimization_barrier((active * upper).astype(jnp.bfloat16)).astype(jnp.float32)
        slot_grad = jnp.sum(carried * hidden, axis=-1)
        scaled = weight[..., None] * carried
        grad_gate = scaled * upper * sigma * (1.0 + gate * (1.0 - sigma))
        grad_upper = scaled * active
        return jnp.concatenate([grad_gate, grad_upper], axis=-1).astype(jnp.bfloat16), slot_grad

    grads, slot_grads = lax.map(per_expert, jnp.arange(EXPERTS, dtype=jnp.int32))
    grad_gate_up = jnp.transpose(grads, (1, 0, 2, 3, 4))
    slot_table = jnp.transpose(slot_grads, (1, 2, 0, 3)).reshape(blocks, EXPERTS * CAP)
    grad_weights = jnp.take_along_axis(slot_table, slot, axis=1).reshape(TOKENS, TOP)
    return grad_gate_up, grad_weights
```

```python
import functools

import jax
import jax.numpy as jnp
from jax import lax
from jax.experimental import pallas as pl
from jax.experimental.pallas import tpu as pltpu
from jax.sharding import PartitionSpec as P

BF = jnp.bfloat16
F32 = jnp.float32
SHARD = 256
TILE = 512
WAVE_TILES = 2
VMEM = 56 * 1024 * 1024


def ring(axis, step):
    pairs = []
    for z in range(4):
        for y in range(4):
            if axis == "y":
                pairs.append((z * 4 + y, z * 4 + (y + step) % 4))
            else:
                pairs.append((z * 4 + y, ((z + step) % 4) * 4 + y))
    return pairs


def along(x, axis, step):
    return lax.ppermute(x, "inner", ring(axis, step))


def along_x(x, step):
    pairs = [(a * 2 + c, ((a + step) % 4) * 2 + c) for a in range(4) for c in range(2)]
    return lax.ppermute(x, "outer", pairs)


def together(*groups):
    return [list(g) for g in lax.optimization_barrier(tuple(tuple(g) for g in groups))]


def params(steps):
    return pltpu.CompilerParams(
        dimension_semantics=("arbitrary",) * steps, vmem_limit_bytes=VMEM
    )


def plan_kernel(routes_ref, weights_ref, out_ref):
    routes = routes_ref[...]
    weights = weights_ref[...].astype(F32)
    tokens = routes.shape[1]
    experts = out_ref.shape[0] * 2
    expert = lax.broadcasted_iota(jnp.int32, (experts, tokens), 0)
    named = jnp.zeros((experts, tokens), F32)
    weight = jnp.zeros((experts, tokens), F32)
    for k in range(routes.shape[0]):
        same = routes[k : k + 1, :] == expert
        named = jnp.where(same, 1.0, named)
        weight = jnp.where(same, weights[k : k + 1, :], weight)
    earlier = lax.broadcasted_iota(jnp.int32, (tokens, tokens), 0)
    later = lax.broadcasted_iota(jnp.int32, (tokens, tokens), 1)
    before = jnp.where(earlier < later, 1.0, 0.0).astype(BF)
    position = jnp.dot(named.astype(BF), before, preferred_element_type=F32)
    position = jnp.where(named > 0.0, position, -1.0)
    for e in range(experts):
        out_ref[e // 2, e % 2 : e % 2 + 1, :] = position[e : e + 1, :]
        out_ref[e // 2, 2 + e % 2 : 3 + e % 2, :] = weight[e : e + 1, :]


def plan(routes, route_weights, n_outer):
    return pl.pallas_call(
        plan_kernel,
        out_shape=jax.ShapeDtypeStruct((n_outer, 4, routes.shape[1]), F32),
        name="plan",
    )(routes, route_weights)


def pick_kernel(routes_ref, grads_ref, out_ref):
    routes = routes_ref[...]
    total = jnp.zeros(routes.shape, F32)
    for o in range(grads_ref.shape[0]):
        for j in range(2):
            total = jnp.where(routes == 2 * o + j, grads_ref[o, j : j + 1, :], total)
    out_ref[...] = total


def pick(routes, grads):
    return pl.pallas_call(
        pick_kernel, out_shape=jax.ShapeDtypeStruct(routes.shape, F32), name="pick"
    )(routes, grads)


def fill_kernel(source_ref, tokens_ref, plan_ref, *rest):
    rows_ref, weight_ref = rest[-2:]
    tokens = plan_ref.shape[-1]
    cap = rows_ref.shape[2]
    slot = lax.broadcasted_iota(jnp.int32, (cap, tokens), 0).astype(F32)
    width = tokens_ref.shape[-1]
    step = 1024
    picks = []
    for j in range(2):
        owned = slot == plan_ref[0, j : j + 1, :]
        picks.append(jnp.where(owned, 1.0, 0.0))
        weight = jnp.sum(
            jnp.where(owned, plan_ref[0, 2 + j : 3 + j, :], 0.0), axis=1, keepdims=True
        )
        weight_ref[j, 0] = jnp.broadcast_to(weight, weight_ref.shape[2:])
    picks = jnp.concatenate(picks, axis=0).astype(BF)
    for c in range(0, width, step):
        rows = jnp.dot(picks, tokens_ref[0, :, c : c + step], preferred_element_type=F32)
        rows_ref[0, 0, :, c : c + step] = rows[:cap].astype(BF)
        rows_ref[1, 0, :, c : c + step] = rows[cap:].astype(BF)


def fill(sources, tokens, plans, cap, earlier=None):
    count, rows, width = tokens.shape
    n_outer = plans.shape[0]
    extra = [] if earlier is None else list(earlier)
    return pl.pallas_call(
        fill_kernel,
        grid_spec=pltpu.PrefetchScalarGridSpec(
            num_scalar_prefetch=1,
            grid=(count,),
            in_specs=[
                pl.BlockSpec((1, rows, width), lambda q, src: (q, 0, 0)),
                pl.BlockSpec((1, 4, rows), lambda q, src: (src[q], 0, 0)),
            ]
            + [pl.BlockSpec(memory_space=pl.ANY)] * len(extra),
            out_specs=[
                pl.BlockSpec((2, 1, cap, width), lambda q, src: (0, src[q], 0, 0)),
                pl.BlockSpec((2, 1, cap, 128), lambda q, src: (0, src[q], 0, 0)),
            ],
        ),
        out_shape=[
            jax.ShapeDtypeStruct((2, n_outer, cap, width), BF),
            jax.ShapeDtypeStruct((2, n_outer, cap, 128), F32),
        ],
        input_output_aliases={3: 0, 4: 1} if extra else {},
        compiler_params=params(1),
        cost_estimate=pl.CostEstimate(
            flops=2 * count * 2 * cap * rows * width,
            bytes_accessed=count * (rows + 2 * cap) * width * 2,
            transcendentals=0,
        ),
        name="fill",
    )(sources, tokens, plans, *extra)


def product(rows, weight):
    return lax.dot_general(
        rows, weight, (((1,), (1,)), ((), ())), preferred_element_type=F32
    )


def backward(total_ref, gate_ref, up_ref, weight_ref, out_ref, sums_ref):
    sources, cap = gate_ref.shape[0], gate_ref.shape[3]
    for s in range(sources):
        at = slice(s * cap, (s + 1) * cap)
        for c in range(0, TILE, 128):
            cols = slice(c, c + 128)
            carried = total_ref[at, cols]
            gate = gate_ref[s, 0, 0, :, cols].astype(F32)
            upper = up_ref[s, 0, 0, :, cols].astype(F32)
            sigma = 0.5 * jnp.tanh(0.5 * gate) + 0.5
            active = gate * sigma
            hidden = (active * upper).astype(BF).astype(F32)
            sums_ref[at, :] += carried * hidden
            scaled = weight_ref[0, at, :] * carried
            out_ref[0, s, :, cols] = (
                scaled * upper * (sigma + active * (1.0 - sigma))
            ).astype(BF)
            out_ref[1, s, :, cols] = (scaled * active).astype(BF)


def out_copies(stage_ref, out_ref, sems, slot, j, tile):
    hid = out_ref.shape[-1] // 2
    return [
        pltpu.make_async_copy(
            stage_ref.at[slot, half],
            out_ref.at[:, j, 0, :, pl.ds(pl.multiple_of(half * hid + tile * TILE, TILE), TILE)],
            sems.at[slot, half],
        )
        for half in range(2)
    ]


def staged(stage_ref, out_ref, sems, j, tile, tiles, first, compute):
    step = j * tiles + tile
    slot = step % 2

    @pl.when(step >= 2)
    def _():
        old = step - 2
        for copy in out_copies(
            stage_ref, out_ref, sems, slot, old // tiles, first + old % tiles
        ):
            copy.wait()

    compute(stage_ref.at[slot])
    for copy in out_copies(stage_ref, out_ref, sems, slot, j, first + tile):
        copy.start()

    @pl.when(step == 2 * tiles - 1)
    def _():
        old = step - 1
        for copy in out_copies(
            stage_ref, out_ref, sems, 1 - slot, old // tiles, first + old % tiles
        ):
            copy.wait()
        for copy in out_copies(stage_ref, out_ref, sems, slot, j, first + tile):
            copy.wait()


QUARTER = 1024


def row_copies(rows_ref, held_ref, sems, j):
    return [
        (
            rows_ref.at[j, :, pl.ds(k * QUARTER, QUARTER)],
            held_ref.at[j, :, pl.ds(k * QUARTER, QUARTER)],
            sems.at[j, k],
        )
        for k in range(held_ref.shape[2] // QUARTER)
    ]


def start_rows(rows_ref, held_ref, sems):
    for e in range(2):
        for copy in row_copies(rows_ref, held_ref, sems, e):
            pltpu.make_async_copy(*copy).start()


def whole_kernel(tiles, rows_ref, w_ref, gate_ref, up_ref, weight_ref, *rest):
    out_ref, sums_ref, total_ref, stage_ref, out_sems, held_ref, sems = rest
    j, tile = pl.program_id(0), pl.program_id(1)

    @pl.when((j == 0) & (tile == 0))
    def _():
        start_rows(rows_ref, held_ref, sems)

    @pl.when(tile == 0)
    def _():
        sums_ref[...] = jnp.zeros_like(sums_ref)

    for k in range(4):

        @pl.when(tile == 0)
        def _(k=k):
            pltpu.make_async_copy(*row_copies(rows_ref, held_ref, sems, j)[k]).wait()

        weight = jnp.concatenate([w_ref[4 * k + i, 0] for i in range(4)], axis=1)
        part = product(held_ref[j, :, k * QUARTER : (k + 1) * QUARTER], weight)
        total_ref[...] = part if k == 0 else total_ref[...] + part

    def compute(slot_ref):
        backward(total_ref, gate_ref, up_ref, weight_ref, slot_ref, sums_ref.at[0])

    staged(stage_ref, out_ref, out_sems, j, tile, tiles, 0, compute)


def whole(rows, w, saved, weights):
    _, slots, width = rows.shape
    sources, _, _, cap, both = saved.shape
    tiles = w.shape[2] // TILE
    shift = both // 2 // TILE
    tile = (sources, 1, 1, cap, TILE)
    return pl.pallas_call(
        functools.partial(whole_kernel, tiles),
        grid=(2, tiles),
        in_specs=[
            pl.BlockSpec(memory_space=pl.ANY),
            pl.BlockSpec((16, 1, TILE, SHARD), lambda j, h: (0, j, h, 0)),
            pl.BlockSpec(tile, lambda j, h: (0, j, 0, 0, h)),
            pl.BlockSpec(tile, lambda j, h: (0, j, 0, 0, h + shift)),
            pl.BlockSpec((1, slots, 128), lambda j, h: (j, 0, 0)),
        ],
        out_specs=[
            pl.BlockSpec(memory_space=pl.ANY),
            pl.BlockSpec((1, slots, 128), lambda j, h: (j, 0, 0)),
        ],
        out_shape=[
            jax.ShapeDtypeStruct(saved.shape, BF),
            jax.ShapeDtypeStruct((2, slots, 128), F32),
        ],
        scratch_shapes=[
            pltpu.VMEM((slots, TILE), F32),
            pltpu.VMEM((2, 2, sources, cap, TILE), BF),
            pltpu.SemaphoreType.DMA((2, 2)),
            pltpu.VMEM(rows.shape, BF),
            pltpu.SemaphoreType.DMA((2, width // QUARTER)),
        ],
        compiler_params=params(2),
        cost_estimate=pl.CostEstimate(
            flops=4 * slots * width * tiles * TILE,
            bytes_accessed=4 * slots * width + 4 * tiles * TILE * (width + 4 * slots),
            transcendentals=2 * slots * tiles * TILE,
        ),
        name="whole",
    )(rows, w, saved, saved, weights)


def columns(ref, j, order_ref, first):
    return jnp.concatenate(
        [
            ref[j, :, pl.ds(pl.multiple_of(order_ref[first + i] * SHARD, SHARD), SHARD)]
            for i in range(4)
        ],
        axis=1,
    )


def most_kernel(order_ref, rows_ref, *rest):
    blocks, (total_ref, held_ref, sems) = rest[:6], rest[6:]
    j, tile = pl.program_id(0), pl.program_id(1)

    @pl.when((j == 0) & (tile == 0))
    def _():
        start_rows(rows_ref, held_ref, sems)

    @pl.when(tile == 0)
    def _():
        for copy in row_copies(rows_ref, held_ref, sems, j):
            pltpu.make_async_copy(*copy).wait()

    for e in range(2):

        @pl.when(j == e)
        def _(e=e):
            for n, w_ref in enumerate(blocks[3 * e : 3 * e + 3]):
                weight = jnp.concatenate([w_ref[i] for i in range(4)], axis=1)
                part = product(columns(held_ref, e, order_ref, 16 * e + 4 * n), weight)
                total_ref[0] = part if n == 0 else total_ref[0] + part


def a_map(tiles, j, h, o):
    return 0, jnp.where(j == 0, h, tiles - 1), 0


def b_map(j, h, o):
    return 0, jnp.where(j == 0, 0, h), 0


def most(order, rows, blocks):
    _, slots, width = rows.shape
    tiles = blocks[0].shape[1] // TILE
    return pl.pallas_call(
        most_kernel,
        grid_spec=pltpu.PrefetchScalarGridSpec(
            num_scalar_prefetch=1,
            grid=(2, tiles),
            in_specs=[pl.BlockSpec(memory_space=pl.ANY)]
            + [pl.BlockSpec((4, TILE, SHARD), functools.partial(a_map, tiles))] * 3
            + [pl.BlockSpec((4, TILE, SHARD), b_map)] * 3,
            out_specs=pl.BlockSpec((1, slots, TILE), lambda j, h, o: (j, 0, h)),
            scratch_shapes=[
                pltpu.VMEM(rows.shape, BF),
                pltpu.SemaphoreType.DMA((2, width // QUARTER)),
            ],
        ),
        out_shape=jax.ShapeDtypeStruct((2, slots, tiles * TILE), F32),
        compiler_params=params(2),
        cost_estimate=pl.CostEstimate(
            flops=4 * slots * width * tiles * TILE * 3 // 4,
            bytes_accessed=4 * slots * width + 2 * tiles * TILE * (2 * width + 4 * slots),
            transcendentals=0,
        ),
        name="most",
    )(order, rows, *blocks)


def last_kernel(first, tiles, order_ref, *rest):
    columns_refs, blocks = rest[:4], rest[4:8]
    gate_ref, up_ref, weight_ref, most_ref, before_ref, plan_ref = rest[8:14]
    out_ref, grads_ref, total_ref, stage_ref, out_sems, sums_ref = rest[15:]
    j, tile = pl.program_id(0), pl.program_id(1)

    @pl.when(tile == 0)
    def _():
        sums_ref[...] = before_ref[0]

    rows = jnp.concatenate([ref[0] for ref in columns_refs], axis=1)
    for e in range(2):

        @pl.when(j == e)
        def _(e=e):
            a_ref, b_ref = blocks[2 * e : 2 * e + 2]
            weight = jnp.concatenate([a_ref[0], a_ref[1], b_ref[0], b_ref[1]], axis=1)
            total_ref[...] = most_ref[0] + product(rows, weight)

    def compute(slot_ref):
        backward(total_ref, gate_ref, up_ref, weight_ref, slot_ref, sums_ref)

    staged(stage_ref, out_ref, out_sems, j, tile, tiles, first, compute)

    @pl.when(tile == tiles - 1)
    def _():
        cap, tokens = gate_ref.shape[3], plan_ref.shape[-1]
        slot = lax.broadcasted_iota(jnp.int32, (cap, tokens), 0).astype(F32)
        for s in range(gate_ref.shape[0]):
            value = jnp.sum(sums_ref[s * cap : (s + 1) * cap, :], axis=1, keepdims=True)
            owned = slot == plan_ref[s, pl.ds(j, 1), :]
            grads_ref[s, pl.ds(j, 1), :] = jnp.sum(
                jnp.where(owned, value, 0.0), axis=0, keepdims=True
            )


def last(order, rows, blocks, saved, weights, partial, before, plans, out):
    _, slots, width = rows.shape
    sources, _, _, cap, both = saved.shape
    tiles = blocks[0].shape[1] // TILE
    shift = both // 2 // TILE
    first = shift - tiles
    tokens = plans.shape[-1]
    tile = (sources, 1, 1, cap, TILE)
    return pl.pallas_call(
        functools.partial(last_kernel, first, tiles),
        grid_spec=pltpu.PrefetchScalarGridSpec(
            num_scalar_prefetch=1,
            grid=(2, tiles),
            in_specs=[
                pl.BlockSpec(
                    (1, slots, SHARD), lambda j, h, o, i=i: (j, 0, o[16 * j + 12 + i])
                )
                for i in range(4)
            ]
            + [pl.BlockSpec((2, TILE, SHARD), functools.partial(a_map, tiles))] * 2
            + [pl.BlockSpec((2, TILE, SHARD), b_map)] * 2
            + [
                pl.BlockSpec(tile, lambda j, h, o: (0, j, 0, 0, first + h)),
                pl.BlockSpec(tile, lambda j, h, o: (0, j, 0, 0, first + h + shift)),
                pl.BlockSpec((1, slots, 128), lambda j, h, o: (j, 0, 0)),
                pl.BlockSpec((1, slots, TILE), lambda j, h, o: (j, 0, h)),
                pl.BlockSpec((1, slots, 128), lambda j, h, o: (j, 0, 0)),
                pl.BlockSpec((sources, 4, tokens), lambda j, h, o: (0, 0, 0)),
                pl.BlockSpec(memory_space=pl.ANY),
            ],
            out_specs=[
                pl.BlockSpec(memory_space=pl.ANY),
                pl.BlockSpec((sources, 2, tokens), lambda j, h, o: (0, 0, 0)),
            ],
            scratch_shapes=[
                pltpu.VMEM((slots, TILE), F32),
                pltpu.VMEM((2, 2, sources, cap, TILE), BF),
                pltpu.SemaphoreType.DMA((2, 2)),
                pltpu.VMEM((slots, 128), F32),
            ],
        ),
        out_shape=[
            jax.ShapeDtypeStruct(saved.shape, BF),
            jax.ShapeDtypeStruct((sources, 2, tokens), F32),
        ],
        input_output_aliases={15: 0},
        compiler_params=params(2),
        cost_estimate=pl.CostEstimate(
            flops=4 * slots * width * tiles * TILE // 4,
            bytes_accessed=2 * slots * width + 2 * tiles * TILE * (width + 12 * slots),
            transcendentals=2 * slots * tiles * TILE,
        ),
        name="last",
    )(
        order, rows, rows, rows, rows, *blocks, saved, saved, weights, partial, before,
        plans, out,
    )


def shards(grad_out, route_weights, routes, saved_gate_up, down_weight):
    n_outer = lax.axis_size("outer")
    cap = saved_gate_up.shape[3]
    hid = down_weight.shape[1]
    split = hid - WAVE_TILES * TILE
    inner, outer = lax.axis_index("inner"), lax.axis_index("outer")
    z, y, x, core = inner // 4, inner % 4, outer // 2, outer % 2

    gathered = lax.all_gather(down_weight[:, :split], "inner", axis=0, tiled=False)

    a, b = down_weight[0, split:], down_weight[1, split:]
    first = [along_x(grad_out, 1), along_x(grad_out, -1)]
    one = [along(a, "y", 1), along(a, "y", -1), along(b, "z", 1), along(b, "z", -1)]
    one += [along(a, "y", 2), along(b, "z", 2)]
    one, first = together(one, first)
    half = grad_out.shape[0] // 2
    second = [along_x(first[0][:half], 1), along_x(first[1][half:], -1)]
    block_a = jnp.stack([a, one[0], one[1], one[4]])
    block_b = jnp.stack([b, one[2], one[3], one[5]])
    three = [
        along(block_a, "z", 1), along(block_a, "z", -1), along(block_b, "y", 1), along(block_b, "y", -1)
    ]

    mine = jnp.stack([grad_out, *first, jnp.concatenate(second)])
    other = lax.ppermute(mine, "outer", [(i, i ^ 1) for i in range(n_outer)])
    mine, named, scales = lax.optimization_barrier((mine, routes.T, route_weights.T))
    plans = lax.all_to_all(
        plan(named, scales, n_outer), "outer", split_axis=0, concat_axis=0, tiled=True
    )
    steps = jnp.array([0, -1, 1, 2], jnp.int32)
    source = ((x + steps) % 4) * 2
    filled = fill(source + core, mine, plans, cap)
    filled = fill(source + 1 - core, other, plans, cap, filled)
    rows = filled[0].reshape(2, n_outer * cap, grad_out.shape[1])
    weights = filled[1].reshape(2, n_outer * cap, 128)
    out, sums = whole(rows, gathered, saved_gate_up, weights)

    three, (out, sums) = together(three, [out, sums])
    four = [
        along(three[0][:2], "z", 1), along(three[1][2:], "z", -1),
        along(three[2][:2], "y", 1), along(three[3][2:], "y", -1),
    ]
    (four,) = together(four)

    near_z, near_y = (z + steps) % 4, (y + steps) % 4
    order = jnp.concatenate(
        [
            (near_z[:, None] * 4 + near_y[None, :]).reshape(-1),
            (near_y[:, None] + near_z[None, :] * 4).reshape(-1),
        ]
    )
    partial = most(order, rows, [block_a, three[0], three[1], block_b, three[2], three[3]])
    out, grads = last(order, rows, four, saved_gate_up, weights, partial, sums, plans, out)
    returned = lax.all_to_all(grads, "outer", split_axis=0, concat_axis=0, tiled=True)
    return (out, pick(routes.T, returned).T)


def solution(mesh):
    in_specs = (
        P(("outer", "inner"), None),
        P(("outer", "inner"), None),
        P(("outer", "inner"), None),
        P(None, "outer", "inner", None, None),
        P("outer", None, "inner"),
    )
    out_specs = (P(None, "outer", "inner", None, None), P(("outer", "inner"), None))
    return jax.shard_map(shards, mesh=mesh, in_specs=in_specs, out_specs=out_specs, check_vma=False)
```

```python
import functools

import jax
import jax.numpy as jnp
from jax import lax
from jax.experimental import pallas as pl
from jax.experimental.pallas import tpu as pltpu
from jax.sharding import PartitionSpec as P

BF = jnp.bfloat16
F32 = jnp.float32
PARTS = 2
SHARD = 256
TILE = 512
WAVE_TILES = 2
VMEM = 56 * 1024 * 1024
MOST_VMEM = 32 * 1024 * 1024
LAST_VMEM = 50 * 1024 * 1024


def ring(axis, step):
    pairs = []
    for z in range(4):
        for y in range(4):
            if axis == "y":
                pairs.append((z * 4 + y, z * 4 + (y + step) % 4))
            else:
                pairs.append((z * 4 + y, ((z + step) % 4) * 4 + y))
    return pairs


def along(x, axis, step):
    return lax.ppermute(x, "inner", ring(axis, step))


def along_x(x):
    pairs = [(a * 2 + c, ((a + 1 - 2 * c) % 4) * 2 + c) for a in range(4) for c in range(2)]
    return lax.ppermute(x, "outer", pairs)


def other_core(x):
    return lax.ppermute(x, "outer", [(i, i ^ 1) for i in range(8)])


def together(*groups):
    return [list(g) for g in lax.optimization_barrier(tuple(tuple(g) for g in groups))]


def params(steps, vmem=VMEM):
    return pltpu.CompilerParams(
        dimension_semantics=("arbitrary",) * steps, vmem_limit_bytes=vmem
    )


def plan_kernel(routes_ref, weights_ref, out_ref):
    routes = routes_ref[...]
    weights = weights_ref[...].astype(F32)
    tokens = routes.shape[1]
    experts = out_ref.shape[0] * 2
    expert = lax.broadcasted_iota(jnp.int32, (experts, tokens), 0)
    named = jnp.zeros((experts, tokens), F32)
    weight = jnp.zeros((experts, tokens), F32)
    for k in range(routes.shape[0]):
        same = routes[k : k + 1, :] == expert
        named = jnp.where(same, 1.0, named)
        weight = jnp.where(same, weights[k : k + 1, :], weight)
    earlier = lax.broadcasted_iota(jnp.int32, (tokens, tokens), 0)
    later = lax.broadcasted_iota(jnp.int32, (tokens, tokens), 1)
    before = jnp.where(earlier < later, 1.0, 0.0).astype(BF)
    position = jnp.dot(named.astype(BF), before, preferred_element_type=F32)
    position = jnp.where(named > 0.0, position, -1.0)
    for e in range(experts):
        out_ref[e // 2, e % 2 : e % 2 + 1, :] = position[e : e + 1, :]
        out_ref[e // 2, 2 + e % 2 : 3 + e % 2, :] = weight[e : e + 1, :]


def plan(routes, route_weights, n_outer):
    return pl.pallas_call(
        plan_kernel,
        out_shape=jax.ShapeDtypeStruct((n_outer, 4, routes.shape[1]), F32),
        name="plan",
    )(routes, route_weights)


def pick_kernel(routes_ref, grads_ref, out_ref):
    routes = routes_ref[...]
    total = jnp.zeros(routes.shape, F32)
    for o in range(grads_ref.shape[0]):
        for j in range(2):
            total = jnp.where(routes == 2 * o + j, grads_ref[o, j : j + 1, :], total)
    out_ref[...] = total


def pick(routes, grads):
    return pl.pallas_call(
        pick_kernel, out_shape=jax.ShapeDtypeStruct(routes.shape, F32), name="pick"
    )(routes, grads)


def fill_block(tokens_ref, plan_ref, rows_ref, weight_ref):
    tokens = plan_ref.shape[-1]
    cap = rows_ref.shape[2]
    slot = lax.broadcasted_iota(jnp.int32, (cap, tokens), 0).astype(F32)
    width = tokens_ref.shape[-1]
    step = 1024
    picks = []
    for j in range(2):
        owned = slot == plan_ref[0, j : j + 1, :]
        picks.append(jnp.where(owned, 1.0, 0.0))
        weight = jnp.sum(
            jnp.where(owned, plan_ref[0, 2 + j : 3 + j, :], 0.0), axis=1, keepdims=True
        )
        weight_ref[j, 0] = jnp.broadcast_to(weight, weight_ref.shape[2:])
    picks = jnp.concatenate(picks, axis=0).astype(BF)
    for c in range(0, width, step):
        rows = jnp.dot(picks, tokens_ref[0, :, c : c + step], preferred_element_type=F32)
        rows_ref[0, 0, :, c : c + step] = rows[:cap].astype(BF)
        rows_ref[1, 0, :, c : c + step] = rows[cap:].astype(BF)


def fill_kernel(starts, source_ref, *refs):
    tokens_refs, (plan_ref, rows_ref, weight_ref) = refs[:-3], refs[-3:]
    q = pl.program_id(0)
    for n, tokens_ref in enumerate(tokens_refs):

        @pl.when((q >= starts[n]) & (q < starts[n + 1]))
        def _(tokens_ref=tokens_ref):
            fill_block(tokens_ref, plan_ref, rows_ref, weight_ref)


def fill(sources, tokens, plans, cap):
    _, rows, width = tokens[0].shape
    starts = [0]
    for part in tokens:
        starts.append(starts[-1] + part.shape[0])
    count = starts[-1]
    return pl.pallas_call(
        functools.partial(fill_kernel, starts),
        grid_spec=pltpu.PrefetchScalarGridSpec(
            num_scalar_prefetch=1,
            grid=(count,),
            in_specs=[
                pl.BlockSpec(
                    (1, rows, width),
                    lambda q, src, lo=starts[n], top=part.shape[0] - 1: (
                        jnp.clip(q - lo, 0, top), 0, 0
                    ),
                )
                for n, part in enumerate(tokens)
            ]
            + [pl.BlockSpec((1, 4, rows), lambda q, src: (src[q], 0, 0))],
            out_specs=[
                pl.BlockSpec((2, 1, cap, width), lambda q, src: (0, src[q], 0, 0)),
                pl.BlockSpec((2, 1, cap, 128), lambda q, src: (0, src[q], 0, 0)),
            ],
        ),
        out_shape=[
            jax.ShapeDtypeStruct((2, count, cap, width), BF),
            jax.ShapeDtypeStruct((2, count, cap, 128), F32),
        ],
        compiler_params=params(1),
        cost_estimate=pl.CostEstimate(
            flops=2 * count * 2 * cap * rows * width,
            bytes_accessed=count * (rows + 2 * cap) * width * 2,
            transcendentals=0,
        ),
        name="fill",
    )(sources, *tokens, plans)


def product(rows, weight):
    return lax.dot_general(
        rows, weight, (((1,), (1,)), ((), ())), preferred_element_type=F32
    )


def backward(total_ref, gate_ref, up_ref, weight_ref, out_ref, sums_ref, sources):
    cap = gate_ref.shape[3]
    for s in sources:
        at = slice(s * cap, (s + 1) * cap)
        weight = weight_ref[0, at, :]
        for c in range(0, TILE, 128):
            cols = slice(c, c + 128)
            carried = total_ref[at, cols]
            gate = gate_ref[s, 0, 0, :, cols].astype(F32)
            upper = up_ref[s, 0, 0, :, cols].astype(F32)
            sigma = 0.5 * jnp.tanh(0.5 * gate) + 0.5
            active = gate * sigma
            hidden = (active * upper).astype(BF).astype(F32)
            part = carried * hidden
            sums = part if c == 0 else sums + part
            scaled = weight * carried
            out_ref[0, s, :, cols] = (
                scaled * upper * (sigma + active * (1.0 - sigma))
            ).astype(BF)
            out_ref[1, s, :, cols] = (scaled * active).astype(BF)
        sums_ref[at, :] += sums


def out_copies(stage_ref, out_ref, sems, slot, j, tile):
    hid = out_ref.shape[-1] // 2
    return [
        pltpu.make_async_copy(
            stage_ref.at[slot, half],
            out_ref.at[:, j, 0, :, pl.ds(pl.multiple_of(half * hid + tile * TILE, TILE), TILE)],
            sems.at[slot, half],
        )
        for half in range(2)
    ]


def staged(stage_ref, out_ref, sems, j, tile, tiles, first, compute):
    step = j * tiles + tile
    slot = step % 2

    @pl.when(step >= 2)
    def _():
        old = step - 2
        for copy in out_copies(
            stage_ref, out_ref, sems, slot, old // tiles, first + old % tiles
        ):
            copy.wait()

    compute(stage_ref.at[slot])
    for copy in out_copies(stage_ref, out_ref, sems, slot, j, first + tile):
        copy.start()

    @pl.when(step == 2 * tiles - 1)
    def _():
        old = step - 1
        for copy in out_copies(
            stage_ref, out_ref, sems, 1 - slot, old // tiles, first + old % tiles
        ):
            copy.wait()
        for copy in out_copies(stage_ref, out_ref, sems, slot, j, first + tile):
            copy.wait()


QUARTER = 1024


def row_copies(rows_ref, held_ref, sems, j):
    return [
        (
            rows_ref.at[j, :, pl.ds(k * QUARTER, QUARTER)],
            held_ref.at[j, :, pl.ds(k * QUARTER, QUARTER)],
            sems.at[j, k],
        )
        for k in range(held_ref.shape[2] // QUARTER)
    ]


def start_rows(rows_ref, held_ref, sems):
    for e in range(2):
        for copy in row_copies(rows_ref, held_ref, sems, e):
            pltpu.make_async_copy(*copy).start()


def whole_kernel(tiles, rows_ref, w_ref, gate_ref, up_ref, weight_ref, *rest):
    out_ref, sums_ref, total_ref, stage_ref, out_sems, held_ref, sems = rest
    j, tile = pl.program_id(0), pl.program_id(1)

    @pl.when((j == 0) & (tile == 0))
    def _():
        start_rows(rows_ref, held_ref, sems)

    @pl.when(tile == 0)
    def _():
        sums_ref[...] = jnp.zeros_like(sums_ref)

    for k in range(4):

        @pl.when(tile == 0)
        def _(k=k):
            pltpu.make_async_copy(*row_copies(rows_ref, held_ref, sems, j)[k]).wait()

        weight = jnp.concatenate([w_ref[4 * k + i, 0] for i in range(4)], axis=1)
        part = product(held_ref[j, :, k * QUARTER : (k + 1) * QUARTER], weight)
        total_ref[...] = part if k == 0 else total_ref[...] + part

    def compute(slot_ref):
        backward(
            total_ref, gate_ref, up_ref, weight_ref, slot_ref, sums_ref.at[0],
            range(gate_ref.shape[0]),
        )

    staged(stage_ref, out_ref, out_sems, j, tile, tiles, 0, compute)


def whole(rows, w, saved, weights):
    _, slots, width = rows.shape
    sources, _, _, cap, both = saved.shape
    tiles = w.shape[2] // TILE
    shift = both // 2 // TILE
    tile = (sources, 1, 1, cap, TILE)
    return pl.pallas_call(
        functools.partial(whole_kernel, tiles),
        grid=(2, tiles),
        in_specs=[
            pl.BlockSpec(memory_space=pl.ANY),
            pl.BlockSpec((16, 1, TILE, SHARD), lambda j, h: (0, j, h, 0)),
            pl.BlockSpec(tile, lambda j, h: (0, j, 0, 0, h)),
            pl.BlockSpec(tile, lambda j, h: (0, j, 0, 0, h + shift)),
            pl.BlockSpec((1, slots, 128), lambda j, h: (j, 0, 0)),
        ],
        out_specs=[
            pl.BlockSpec(memory_space=pl.ANY),
            pl.BlockSpec((1, slots, 128), lambda j, h: (j, 0, 0)),
        ],
        out_shape=[
            jax.ShapeDtypeStruct(saved.shape, BF),
            jax.ShapeDtypeStruct((2, slots, 128), F32),
        ],
        scratch_shapes=[
            pltpu.VMEM((slots, TILE), F32),
            pltpu.VMEM((2, 2, sources, cap, TILE), BF),
            pltpu.SemaphoreType.DMA((2, 2)),
            pltpu.VMEM(rows.shape, BF),
            pltpu.SemaphoreType.DMA((2, width // QUARTER)),
        ],
        compiler_params=params(2),
        cost_estimate=pl.CostEstimate(
            flops=4 * slots * width * tiles * TILE,
            bytes_accessed=4 * slots * width + 4 * tiles * TILE * (width + 4 * slots),
            transcendentals=2 * slots * tiles * TILE,
        ),
        name="whole",
    )(rows, w, saved, saved, weights)


def columns(ref, j, order_ref, first):
    return jnp.concatenate(
        [
            ref[j, :, pl.ds(pl.multiple_of(order_ref[first + i] * SHARD, SHARD), SHARD)]
            for i in range(4)
        ],
        axis=1,
    )


def most_kernel(order_ref, rows_ref, *rest):
    blocks, (total_ref, held_ref, sems) = rest[:6], rest[6:]
    j, tile = pl.program_id(0), pl.program_id(1)

    @pl.when((j == 0) & (tile == 0))
    def _():
        start_rows(rows_ref, held_ref, sems)

    @pl.when(tile == 0)
    def _():
        for copy in row_copies(rows_ref, held_ref, sems, j):
            pltpu.make_async_copy(*copy).wait()

    for e in range(2):

        @pl.when(j == e)
        def _(e=e):
            for n, w_ref in enumerate(blocks[3 * e : 3 * e + 3]):
                weight = jnp.concatenate([w_ref[i] for i in range(4)], axis=1)
                part = product(columns(held_ref, e, order_ref, 16 * e + 4 * n), weight)
                total_ref[0] = part if n == 0 else total_ref[0] + part


def a_map(tiles, j, h, o):
    return 0, jnp.where(j == 0, h, tiles - 1), 0


def b_map(j, h, o):
    return 0, jnp.where(j == 0, 0, h), 0


def most(order, rows, blocks):
    _, slots, width = rows.shape
    tiles = blocks[0].shape[1] // TILE
    return pl.pallas_call(
        most_kernel,
        grid_spec=pltpu.PrefetchScalarGridSpec(
            num_scalar_prefetch=1,
            grid=(2, tiles),
            in_specs=[pl.BlockSpec(memory_space=pl.ANY)]
            + [pl.BlockSpec((4, TILE, SHARD), functools.partial(a_map, tiles))] * 3
            + [pl.BlockSpec((4, TILE, SHARD), b_map)] * 3,
            out_specs=pl.BlockSpec((1, slots, TILE), lambda j, h, o: (j, 0, h)),
            scratch_shapes=[
                pltpu.VMEM(rows.shape, BF),
                pltpu.SemaphoreType.DMA((2, width // QUARTER)),
            ],
        ),
        out_shape=jax.ShapeDtypeStruct((2, slots, tiles * TILE), F32),
        compiler_params=params(2, MOST_VMEM),
        cost_estimate=pl.CostEstimate(
            flops=4 * slots * width * tiles * TILE * 3 // 4,
            bytes_accessed=4 * slots * width + 2 * tiles * TILE * (2 * width + 4 * slots),
            transcendentals=0,
        ),
        name="most",
    )(order, rows, *blocks)


def last_kernel(first, tiles, order_ref, *rest):
    columns_refs, blocks = rest[:4], rest[4:8]
    gate_ref, up_ref, weight_ref, most_ref, before_ref, plan_ref = rest[8:14]
    out_ref, grads_ref, total_ref, stage_ref, out_sems, sums_ref = rest[15:]
    j, tile = pl.program_id(0), pl.program_id(1)

    @pl.when(tile == 0)
    def _():
        sums_ref[...] = before_ref[0]

    sources, cap = gate_ref.shape[0], gate_ref.shape[3]
    group = sources // PARTS

    def compute(slot_ref):
        for e in range(2):

            @pl.when(j == e)
            def _(e=e):
                a_ref, b_ref = blocks[2 * e : 2 * e + 2]
                weight = jnp.concatenate([a_ref[0], a_ref[1], b_ref[0], b_ref[1]], axis=1)

                def multiply(n):
                    at = slice(n * group * cap, (n + 1) * group * cap)
                    rows = jnp.concatenate([ref[0, at, :] for ref in columns_refs], axis=1)
                    total_ref[at, :] = most_ref[0, at, :] + product(rows, weight)

                multiply(0)
                for n in range(PARTS):
                    if n + 1 < PARTS:
                        multiply(n + 1)
                    backward(
                        total_ref, gate_ref, up_ref, weight_ref, slot_ref, sums_ref,
                        range(n * group, (n + 1) * group),
                    )

    staged(stage_ref, out_ref, out_sems, j, tile, tiles, first, compute)

    @pl.when(tile == tiles - 1)
    def _():
        cap, tokens = gate_ref.shape[3], plan_ref.shape[-1]
        slot = lax.broadcasted_iota(jnp.int32, (cap, tokens), 0).astype(F32)
        for s in range(gate_ref.shape[0]):
            value = jnp.sum(sums_ref[s * cap : (s + 1) * cap, :], axis=1, keepdims=True)
            owned = slot == plan_ref[s, pl.ds(j, 1), :]
            grads_ref[s, pl.ds(j, 1), :] = jnp.sum(
                jnp.where(owned, value, 0.0), axis=0, keepdims=True
            )


def last(order, rows, blocks, saved, weights, partial, before, plans, out):
    _, slots, width = rows.shape
    sources, _, _, cap, both = saved.shape
    tiles = blocks[0].shape[1] // TILE
    shift = both // 2 // TILE
    first = shift - tiles
    tokens = plans.shape[-1]
    tile = (sources, 1, 1, cap, TILE)
    return pl.pallas_call(
        functools.partial(last_kernel, first, tiles),
        grid_spec=pltpu.PrefetchScalarGridSpec(
            num_scalar_prefetch=1,
            grid=(2, tiles),
            in_specs=[
                pl.BlockSpec(
                    (1, slots, SHARD), lambda j, h, o, i=i: (j, 0, o[16 * j + 12 + i])
                )
                for i in range(4)
            ]
            + [pl.BlockSpec((2, TILE, SHARD), functools.partial(a_map, tiles))] * 2
            + [pl.BlockSpec((2, TILE, SHARD), b_map)] * 2
            + [
                pl.BlockSpec(tile, lambda j, h, o: (0, j, 0, 0, first + h)),
                pl.BlockSpec(tile, lambda j, h, o: (0, j, 0, 0, first + h + shift)),
                pl.BlockSpec((1, slots, 128), lambda j, h, o: (j, 0, 0)),
                pl.BlockSpec((1, slots, TILE), lambda j, h, o: (j, 0, h)),
                pl.BlockSpec((1, slots, 128), lambda j, h, o: (j, 0, 0)),
                pl.BlockSpec((sources, 4, tokens), lambda j, h, o: (0, 0, 0)),
                pl.BlockSpec(memory_space=pl.ANY),
            ],
            out_specs=[
                pl.BlockSpec(memory_space=pl.ANY),
                pl.BlockSpec((sources, 2, tokens), lambda j, h, o: (0, 0, 0)),
            ],
            scratch_shapes=[
                pltpu.VMEM((slots, TILE), F32),
                pltpu.VMEM((2, 2, sources, cap, TILE), BF),
                pltpu.SemaphoreType.DMA((2, 2)),
                pltpu.VMEM((slots, 128), F32),
            ],
        ),
        out_shape=[
            jax.ShapeDtypeStruct(saved.shape, BF),
            jax.ShapeDtypeStruct((sources, 2, tokens), F32),
        ],
        input_output_aliases={15: 0},
        compiler_params=params(2, LAST_VMEM),
        cost_estimate=pl.CostEstimate(
            flops=4 * slots * width * tiles * TILE // 4,
            bytes_accessed=2 * slots * width + 2 * tiles * TILE * (width + 12 * slots),
            transcendentals=2 * slots * tiles * TILE,
        ),
        name="last",
    )(
        order, rows, rows, rows, rows, *blocks, saved, saved, weights, partial, before,
        plans, out,
    )


def halves_kernel(*refs):
    blocks, parts, held, sems = refs[:4], refs[4:8], refs[8:12], refs[12]
    reads = [
        pltpu.make_async_copy(blocks[n].at[pl.ds(2 * (n % 2), 2)], held[n], sems.at[0, n])
        for n in range(4)
    ]
    writes = [pltpu.make_async_copy(held[n], parts[n], sems.at[1, n]) for n in range(4)]
    for copy in reads:
        copy.start()
    for read, write in zip(reads, writes):
        read.wait()
        write.start()
    for copy in writes:
        copy.wait()


def halves(blocks):
    _, tall, wide = blocks[0].shape
    return pl.pallas_call(
        halves_kernel,
        in_specs=[pl.BlockSpec(memory_space=pl.ANY)] * 4,
        out_specs=[pl.BlockSpec(memory_space=pl.ANY)] * 4,
        out_shape=[jax.ShapeDtypeStruct((2, tall, wide), BF)] * 4,
        scratch_shapes=[pltpu.VMEM((2, tall, wide), BF)] * 4
        + [pltpu.SemaphoreType.DMA((2, 4))],
        compiler_params=pltpu.CompilerParams(vmem_limit_bytes=VMEM),
        name="halves",
    )(*blocks)


def shards(grad_out, route_weights, routes, saved_gate_up, down_weight):
    n_outer = lax.axis_size("outer")
    cap = saved_gate_up.shape[3]
    hid = down_weight.shape[1]
    split = hid - WAVE_TILES * TILE
    inner, outer = lax.axis_index("inner"), lax.axis_index("outer")
    z, y, x, core = inner // 4, inner % 4, outer // 2, outer % 2
    steps = jnp.array([0, -1, 1, 2], jnp.int32)

    gathered = lax.all_gather(down_weight[:, :split], "inner", axis=0, tiled=False)

    a, b = down_weight[0, split:], down_weight[1, split:]
    pair = jnp.stack([grad_out, other_core(grad_out)])
    pair, (a, b) = lax.optimization_barrier((pair, (a, b)))
    one = [along(a, "y", 1), along(a, "y", -1), along(b, "z", 1), along(b, "z", -1)]
    near = along_x(pair)
    one, (near,) = together(one, [near])
    two = [along(one[0], "y", 1), along(one[3], "z", -1)]
    far = along_x(near[0])
    near_other = other_core(near)
    two, (far, near_other, named, scales) = together(
        two, [far, near_other, routes.T, route_weights.T]
    )
    block_a = jnp.stack([a, one[0], one[1], two[0]])
    block_b = jnp.stack([b, one[2], one[3], two[1]])
    three = [
        along(block_a, "z", 1), along(block_a, "z", -1), along(block_b, "y", 1), along(block_b, "y", -1)
    ]

    far_other = other_core(far)
    plans = lax.all_to_all(
        plan(named, scales, n_outer), "outer", split_axis=0, concat_axis=0, tiled=True
    )
    came, went = (x + 2 * core - 1) % 4, (x + 1 - 2 * core) % 4
    opposite = (x + 2) % 4
    source = jnp.stack(
        [
            2 * x + core, 2 * x + 1 - core, 2 * came + core, 2 * came + 1 - core,
            2 * went + 1 - core, 2 * went + core, 2 * opposite + core, 2 * opposite + 1 - core,
        ]
    )
    filled = fill(source, [pair, near, near_other, far[None], far_other[None]], plans, cap)
    rows = filled[0].reshape(2, n_outer * cap, grad_out.shape[1])
    weights = filled[1].reshape(2, n_outer * cap, 128)
    out, sums = whole(rows, gathered, saved_gate_up, weights)

    three, (out, sums) = together(three, [out, sums])
    parts = halves(three)
    four = [
        along(parts[0], "z", 1), along(parts[1], "z", -1),
        along(parts[2], "y", 1), along(parts[3], "y", -1),
    ]
    (four,) = together(four)

    near_z, near_y = (z + steps) % 4, (y + steps) % 4
    order = jnp.concatenate(
        [
            (near_z[:, None] * 4 + near_y[None, :]).reshape(-1),
            (near_y[:, None] + near_z[None, :] * 4).reshape(-1),
        ]
    )
    partial = most(order, rows, [block_a, three[0], three[1], block_b, three[2], three[3]])
    out, grads = last(order, rows, four, saved_gate_up, weights, partial, sums, plans, out)
    returned = lax.all_to_all(grads, "outer", split_axis=0, concat_axis=0, tiled=True)
    return (out, pick(routes.T, returned).T)


def solution(mesh):
    in_specs = (
        P(("outer", "inner"), None),
        P(("outer", "inner"), None),
        P(("outer", "inner"), None),
        P(None, "outer", "inner", None, None),
        P("outer", None, "inner"),
    )
    out_specs = (P(None, "outer", "inner", None, None), P(("outer", "inner"), None))
    return jax.shard_map(shards, mesh=mesh, in_specs=in_specs, out_specs=out_specs, check_vma=False)
```

```python
import functools

import jax
import jax.numpy as jnp
from jax import lax
from jax.experimental import pallas as pl
from jax.experimental.pallas import tpu as pltpu
from jax.sharding import PartitionSpec as P

BF = jnp.bfloat16
F32 = jnp.float32
PARTS = 2
SHARD = 256
TILE = 512
WAVE_TILES = 2
VMEM = 56 * 1024 * 1024
MOST_VMEM = 32 * 1024 * 1024
LAST_VMEM = 50 * 1024 * 1024


def ring(axis, step):
    pairs = []
    for z in range(4):
        for y in range(4):
            if axis == "y":
                pairs.append((z * 4 + y, z * 4 + (y + step) % 4))
            else:
                pairs.append((z * 4 + y, ((z + step) % 4) * 4 + y))
    return pairs


def along(x, axis, step):
    return lax.ppermute(x, "inner", ring(axis, step))


def along_x(x):
    pairs = [(a * 2 + c, ((a + 1 - 2 * c) % 4) * 2 + c) for a in range(4) for c in range(2)]
    return lax.ppermute(x, "outer", pairs)


def other_core(x):
    return lax.ppermute(x, "outer", [(i, i ^ 1) for i in range(8)])


def together(*groups):
    return [list(g) for g in lax.optimization_barrier(tuple(tuple(g) for g in groups))]


def params(steps, vmem=VMEM):
    return pltpu.CompilerParams(
        dimension_semantics=("arbitrary",) * steps, vmem_limit_bytes=vmem
    )


def plan_kernel(routes_ref, weights_ref, out_ref):
    routes = routes_ref[...]
    weights = weights_ref[...].astype(F32)
    tokens = routes.shape[1]
    experts = out_ref.shape[0] * 2
    expert = lax.broadcasted_iota(jnp.int32, (experts, tokens), 0)
    named = jnp.zeros((experts, tokens), F32)
    weight = jnp.zeros((experts, tokens), F32)
    for k in range(routes.shape[0]):
        same = routes[k : k + 1, :] == expert
        named = jnp.where(same, 1.0, named)
        weight = jnp.where(same, weights[k : k + 1, :], weight)
    earlier = lax.broadcasted_iota(jnp.int32, (tokens, tokens), 0)
    later = lax.broadcasted_iota(jnp.int32, (tokens, tokens), 1)
    before = jnp.where(earlier < later, 1.0, 0.0).astype(BF)
    position = jnp.dot(named.astype(BF), before, preferred_element_type=F32)
    position = jnp.where(named > 0.0, position, -1.0)
    for e in range(experts):
        out_ref[e // 2, e % 2 : e % 2 + 1, :] = position[e : e + 1, :]
        out_ref[e // 2, 2 + e % 2 : 3 + e % 2, :] = weight[e : e + 1, :]


def plan(routes, route_weights, n_outer):
    return pl.pallas_call(
        plan_kernel,
        out_shape=jax.ShapeDtypeStruct((n_outer, 4, routes.shape[1]), F32),
        name="plan",
    )(routes, route_weights)


def pick_kernel(routes_ref, grads_ref, out_ref):
    routes = routes_ref[...]
    total = jnp.zeros(routes.shape, F32)
    for o in range(grads_ref.shape[0]):
        for j in range(2):
            total = jnp.where(routes == 2 * o + j, grads_ref[o, j : j + 1, :], total)
    out_ref[...] = total


def pick(routes, grads):
    return pl.pallas_call(
        pick_kernel, out_shape=jax.ShapeDtypeStruct(routes.shape, F32), name="pick"
    )(routes, grads)


def fill_block(tokens_ref, plan_ref, rows_ref, weight_ref):
    tokens = plan_ref.shape[-1]
    cap = rows_ref.shape[2]
    slot = lax.broadcasted_iota(jnp.int32, (cap, tokens), 0).astype(F32)
    width = tokens_ref.shape[-1]
    step = 1024
    picks = []
    for j in range(2):
        owned = slot == plan_ref[0, j : j + 1, :]
        picks.append(jnp.where(owned, 1.0, 0.0))
        weight = jnp.sum(
            jnp.where(owned, plan_ref[0, 2 + j : 3 + j, :], 0.0), axis=1, keepdims=True
        )
        weight_ref[j, 0] = jnp.broadcast_to(weight, weight_ref.shape[2:])
    picks = jnp.concatenate(picks, axis=0).astype(BF)
    for c in range(0, width, step):
        rows = jnp.dot(picks, tokens_ref[0, :, c : c + step], preferred_element_type=F32)
        rows_ref[0, 0, :, c : c + step] = rows[:cap].astype(BF)
        rows_ref[1, 0, :, c : c + step] = rows[cap:].astype(BF)


def fill_kernel(starts, source_ref, *refs):
    tokens_refs, (plan_ref, rows_ref, weight_ref) = refs[:-3], refs[-3:]
    q = pl.program_id(0)
    for n, tokens_ref in enumerate(tokens_refs):

        @pl.when((q >= starts[n]) & (q < starts[n + 1]))
        def _(tokens_ref=tokens_ref):
            fill_block(tokens_ref, plan_ref, rows_ref, weight_ref)


def fill(sources, tokens, plans, cap):
    _, rows, width = tokens[0].shape
    starts = [0]
    for part in tokens:
        starts.append(starts[-1] + part.shape[0])
    count = starts[-1]
    return pl.pallas_call(
        functools.partial(fill_kernel, starts),
        grid_spec=pltpu.PrefetchScalarGridSpec(
            num_scalar_prefetch=1,
            grid=(count,),
            in_specs=[
                pl.BlockSpec(
                    (1, rows, width),
                    lambda q, src, lo=starts[n], top=part.shape[0] - 1: (
                        jnp.clip(q - lo, 0, top), 0, 0
                    ),
                )
                for n, part in enumerate(tokens)
            ]
            + [pl.BlockSpec((1, 4, rows), lambda q, src: (src[q], 0, 0))],
            out_specs=[
                pl.BlockSpec((2, 1, cap, width), lambda q, src: (0, src[q], 0, 0)),
                pl.BlockSpec((2, 1, cap, 128), lambda q, src: (0, src[q], 0, 0)),
            ],
        ),
        out_shape=[
            jax.ShapeDtypeStruct((2, count, cap, width), BF),
            jax.ShapeDtypeStruct((2, count, cap, 128), F32),
        ],
        compiler_params=params(1),
        cost_estimate=pl.CostEstimate(
            flops=2 * count * 2 * cap * rows * width,
            bytes_accessed=count * (rows + 2 * cap) * width * 2,
            transcendentals=0,
        ),
        name="fill",
    )(sources, *tokens, plans)


def product(rows, weight):
    return lax.dot_general(
        rows, weight, (((1,), (1,)), ((), ())), preferred_element_type=F32
    )


def backward(total_ref, gate_ref, up_ref, weight_ref, out_ref, sums_ref, sources):
    cap = gate_ref.shape[3]
    for s in sources:
        at = slice(s * cap, (s + 1) * cap)
        weight = weight_ref[0, at, :]
        for c in range(0, TILE, 128):
            cols = slice(c, c + 128)
            carried = total_ref[at, cols]
            gate = gate_ref[s, 0, 0, :, cols].astype(F32)
            upper = up_ref[s, 0, 0, :, cols].astype(F32)
            sigma = 0.5 * jnp.tanh(0.5 * gate) + 0.5
            active = gate * sigma
            hidden = (active * upper).astype(BF).astype(F32)
            part = carried * hidden
            sums = part if c == 0 else sums + part
            scaled = weight * carried
            out_ref[0, s, :, cols] = (
                scaled * upper * (sigma + active * (1.0 - sigma))
            ).astype(BF)
            out_ref[1, s, :, cols] = (scaled * active).astype(BF)
        sums_ref[at, :] += sums


def out_copies(stage_ref, out_ref, sems, slot, j, tile):
    hid = out_ref.shape[-1] // 2
    return [
        pltpu.make_async_copy(
            stage_ref.at[slot, half],
            out_ref.at[:, j, 0, :, pl.ds(pl.multiple_of(half * hid + tile * TILE, TILE), TILE)],
            sems.at[slot, half],
        )
        for half in range(2)
    ]


def staged(stage_ref, out_ref, sems, j, tile, tiles, first, compute):
    step = j * tiles + tile
    slot = step % 2

    @pl.when(step >= 2)
    def _():
        old = step - 2
        for copy in out_copies(
            stage_ref, out_ref, sems, slot, old // tiles, first + old % tiles
        ):
            copy.wait()

    compute(stage_ref.at[slot])
    for copy in out_copies(stage_ref, out_ref, sems, slot, j, first + tile):
        copy.start()

    @pl.when(step == 2 * tiles - 1)
    def _():
        old = step - 1
        for copy in out_copies(
            stage_ref, out_ref, sems, 1 - slot, old // tiles, first + old % tiles
        ):
            copy.wait()
        for copy in out_copies(stage_ref, out_ref, sems, slot, j, first + tile):
            copy.wait()


QUARTER = 1024


def row_copies(rows_ref, held_ref, sems, j):
    return [
        (
            rows_ref.at[j, :, pl.ds(k * QUARTER, QUARTER)],
            held_ref.at[j, :, pl.ds(k * QUARTER, QUARTER)],
            sems.at[j, k],
        )
        for k in range(held_ref.shape[2] // QUARTER)
    ]


def start_rows(rows_ref, held_ref, sems):
    for e in range(2):
        for copy in row_copies(rows_ref, held_ref, sems, e):
            pltpu.make_async_copy(*copy).start()


def whole_kernel(tiles, rows_ref, w_ref, gate_ref, up_ref, weight_ref, *rest):
    out_ref, sums_ref, total_ref, stage_ref, out_sems, held_ref, sems = rest
    j, tile = pl.program_id(0), pl.program_id(1)

    @pl.when((j == 0) & (tile == 0))
    def _():
        start_rows(rows_ref, held_ref, sems)

    @pl.when(tile == 0)
    def _():
        sums_ref[...] = jnp.zeros_like(sums_ref)

    for k in range(4):

        @pl.when(tile == 0)
        def _(k=k):
            pltpu.make_async_copy(*row_copies(rows_ref, held_ref, sems, j)[k]).wait()

        weight = jnp.concatenate([w_ref[4 * k + i, 0] for i in range(4)], axis=1)
        part = product(held_ref[j, :, k * QUARTER : (k + 1) * QUARTER], weight)
        total_ref[...] = part if k == 0 else total_ref[...] + part

    def compute(slot_ref):
        backward(
            total_ref, gate_ref, up_ref, weight_ref, slot_ref, sums_ref.at[0],
            range(gate_ref.shape[0]),
        )

    staged(stage_ref, out_ref, out_sems, j, tile, tiles, 0, compute)


def whole(rows, w, saved, weights):
    _, slots, width = rows.shape
    sources, _, _, cap, both = saved.shape
    tiles = w.shape[2] // TILE
    shift = both // 2 // TILE
    tile = (sources, 1, 1, cap, TILE)
    return pl.pallas_call(
        functools.partial(whole_kernel, tiles),
        grid=(2, tiles),
        in_specs=[
            pl.BlockSpec(memory_space=pl.ANY),
            pl.BlockSpec((16, 1, TILE, SHARD), lambda j, h: (0, j, h, 0)),
            pl.BlockSpec(tile, lambda j, h: (0, j, 0, 0, h)),
            pl.BlockSpec(tile, lambda j, h: (0, j, 0, 0, h + shift)),
            pl.BlockSpec((1, slots, 128), lambda j, h: (j, 0, 0)),
        ],
        out_specs=[
            pl.BlockSpec(memory_space=pl.ANY),
            pl.BlockSpec((1, slots, 128), lambda j, h: (j, 0, 0)),
        ],
        out_shape=[
            jax.ShapeDtypeStruct(saved.shape, BF),
            jax.ShapeDtypeStruct((2, slots, 128), F32),
        ],
        scratch_shapes=[
            pltpu.VMEM((slots, TILE), F32),
            pltpu.VMEM((2, 2, sources, cap, TILE), BF),
            pltpu.SemaphoreType.DMA((2, 2)),
            pltpu.VMEM(rows.shape, BF),
            pltpu.SemaphoreType.DMA((2, width // QUARTER)),
        ],
        compiler_params=params(2),
        cost_estimate=pl.CostEstimate(
            flops=4 * slots * width * tiles * TILE,
            bytes_accessed=4 * slots * width + 4 * tiles * TILE * (width + 4 * slots),
            transcendentals=2 * slots * tiles * TILE,
        ),
        name="whole",
    )(rows, w, saved, saved, weights)


def columns(ref, j, order_ref, first):
    return jnp.concatenate(
        [
            ref[j, :, pl.ds(pl.multiple_of(order_ref[first + i] * SHARD, SHARD), SHARD)]
            for i in range(4)
        ],
        axis=1,
    )


def most_kernel(order_ref, rows_ref, *rest):
    blocks, (total_ref, held_ref, sems) = rest[:6], rest[6:]
    j, tile = pl.program_id(0), pl.program_id(1)

    @pl.when((j == 0) & (tile == 0))
    def _():
        start_rows(rows_ref, held_ref, sems)

    @pl.when(tile == 0)
    def _():
        for copy in row_copies(rows_ref, held_ref, sems, j):
            pltpu.make_async_copy(*copy).wait()

    for e in range(2):

        @pl.when(j == e)
        def _(e=e):
            for n, w_ref in enumerate(blocks[3 * e : 3 * e + 3]):
                weight = jnp.concatenate([w_ref[i] for i in range(4)], axis=1)
                part = product(columns(held_ref, e, order_ref, 16 * e + 4 * n), weight)
                total_ref[0] = part if n == 0 else total_ref[0] + part


def a_map(tiles, j, h, o):
    return 0, jnp.where(j == 0, h, tiles - 1), 0


def b_map(j, h, o):
    return 0, jnp.where(j == 0, 0, h), 0


def most(order, rows, blocks):
    _, slots, width = rows.shape
    tiles = blocks[0].shape[1] // TILE
    return pl.pallas_call(
        most_kernel,
        grid_spec=pltpu.PrefetchScalarGridSpec(
            num_scalar_prefetch=1,
            grid=(2, tiles),
            in_specs=[pl.BlockSpec(memory_space=pl.ANY)]
            + [pl.BlockSpec((4, TILE, SHARD), functools.partial(a_map, tiles))] * 3
            + [pl.BlockSpec((4, TILE, SHARD), b_map)] * 3,
            out_specs=pl.BlockSpec((1, slots, TILE), lambda j, h, o: (j, 0, h)),
            scratch_shapes=[
                pltpu.VMEM(rows.shape, BF),
                pltpu.SemaphoreType.DMA((2, width // QUARTER)),
            ],
        ),
        out_shape=jax.ShapeDtypeStruct((2, slots, tiles * TILE), F32),
        compiler_params=params(2, MOST_VMEM),
        cost_estimate=pl.CostEstimate(
            flops=4 * slots * width * tiles * TILE * 3 // 4,
            bytes_accessed=4 * slots * width + 2 * tiles * TILE * (2 * width + 4 * slots),
            transcendentals=0,
        ),
        name="most",
    )(order, rows, *blocks)


def last_kernel(first, tiles, order_ref, *rest):
    columns_refs, blocks = rest[:4], rest[4:8]
    gate_ref, up_ref, weight_ref, most_ref, before_ref, plan_ref = rest[8:14]
    out_ref, grads_ref, total_ref, stage_ref, out_sems, sums_ref = rest[15:]
    j, tile = pl.program_id(0), pl.program_id(1)

    @pl.when(tile == 0)
    def _():
        sums_ref[...] = before_ref[0]

    sources, cap = gate_ref.shape[0], gate_ref.shape[3]
    group = sources // PARTS

    def compute(slot_ref):
        for e in range(2):

            @pl.when(j == e)
            def _(e=e):
                a_ref, b_ref = blocks[2 * e : 2 * e + 2]
                weight = jnp.concatenate([a_ref[0], a_ref[1], b_ref[0], b_ref[1]], axis=1)

                def multiply(n):
                    at = slice(n * group * cap, (n + 1) * group * cap)
                    rows = jnp.concatenate([ref[0, at, :] for ref in columns_refs], axis=1)
                    total_ref[at, :] = most_ref[0, at, :] + product(rows, weight)

                multiply(0)
                for n in range(PARTS):
                    if n + 1 < PARTS:
                        multiply(n + 1)
                    backward(
                        total_ref, gate_ref, up_ref, weight_ref, slot_ref, sums_ref,
                        range(n * group, (n + 1) * group),
                    )

    staged(stage_ref, out_ref, out_sems, j, tile, tiles, first, compute)

    @pl.when(tile == tiles - 1)
    def _():
        cap, tokens = gate_ref.shape[3], plan_ref.shape[-1]
        slot = lax.broadcasted_iota(jnp.int32, (cap, tokens), 0).astype(F32)
        for s in range(gate_ref.shape[0]):
            value = jnp.sum(sums_ref[s * cap : (s + 1) * cap, :], axis=1, keepdims=True)
            owned = slot == plan_ref[s, pl.ds(j, 1), :]
            grads_ref[s, pl.ds(j, 1), :] = jnp.sum(
                jnp.where(owned, value, 0.0), axis=0, keepdims=True
            )


def last(order, rows, blocks, saved, weights, partial, before, plans, out):
    _, slots, width = rows.shape
    sources, _, _, cap, both = saved.shape
    tiles = blocks[0].shape[1] // TILE
    shift = both // 2 // TILE
    first = shift - tiles
    tokens = plans.shape[-1]
    tile = (sources, 1, 1, cap, TILE)
    return pl.pallas_call(
        functools.partial(last_kernel, first, tiles),
        grid_spec=pltpu.PrefetchScalarGridSpec(
            num_scalar_prefetch=1,
            grid=(2, tiles),
            in_specs=[
                pl.BlockSpec(
                    (1, slots, SHARD), lambda j, h, o, i=i: (j, 0, o[16 * j + 12 + i])
                )
                for i in range(4)
            ]
            + [pl.BlockSpec((2, TILE, SHARD), functools.partial(a_map, tiles))] * 2
            + [pl.BlockSpec((2, TILE, SHARD), b_map)] * 2
            + [
                pl.BlockSpec(tile, lambda j, h, o: (0, j, 0, 0, first + h)),
                pl.BlockSpec(tile, lambda j, h, o: (0, j, 0, 0, first + h + shift)),
                pl.BlockSpec((1, slots, 128), lambda j, h, o: (j, 0, 0)),
                pl.BlockSpec((1, slots, TILE), lambda j, h, o: (j, 0, h)),
                pl.BlockSpec((1, slots, 128), lambda j, h, o: (j, 0, 0)),
                pl.BlockSpec((sources, 4, tokens), lambda j, h, o: (0, 0, 0)),
                pl.BlockSpec(memory_space=pl.ANY),
            ],
            out_specs=[
                pl.BlockSpec(memory_space=pl.ANY),
                pl.BlockSpec((sources, 2, tokens), lambda j, h, o: (0, 0, 0)),
            ],
            scratch_shapes=[
                pltpu.VMEM((slots, TILE), F32),
                pltpu.VMEM((2, 2, sources, cap, TILE), BF),
                pltpu.SemaphoreType.DMA((2, 2)),
                pltpu.VMEM((slots, 128), F32),
            ],
        ),
        out_shape=[
            jax.ShapeDtypeStruct(saved.shape, BF),
            jax.ShapeDtypeStruct((sources, 2, tokens), F32),
        ],
        input_output_aliases={15: 0},
        compiler_params=params(2, LAST_VMEM),
        cost_estimate=pl.CostEstimate(
            flops=4 * slots * width * tiles * TILE // 4,
            bytes_accessed=2 * slots * width + 2 * tiles * TILE * (width + 12 * slots),
            transcendentals=2 * slots * tiles * TILE,
        ),
        name="last",
    )(
        order, rows, rows, rows, rows, *blocks, saved, saved, weights, partial, before,
        plans, out,
    )


def halves_kernel(*refs):
    blocks, parts, held, sems = refs[:4], refs[4:8], refs[8:12], refs[12]
    reads = [
        pltpu.make_async_copy(blocks[n].at[pl.ds(2 * (n % 2), 2)], held[n], sems.at[0, n])
        for n in range(4)
    ]
    writes = [pltpu.make_async_copy(held[n], parts[n], sems.at[1, n]) for n in range(4)]
    for copy in reads:
        copy.start()
    for read, write in zip(reads, writes):
        read.wait()
        write.start()
    for copy in writes:
        copy.wait()


def halves(blocks):
    _, tall, wide = blocks[0].shape
    return pl.pallas_call(
        halves_kernel,
        in_specs=[pl.BlockSpec(memory_space=pl.ANY)] * 4,
        out_specs=[pl.BlockSpec(memory_space=pl.ANY)] * 4,
        out_shape=[jax.ShapeDtypeStruct((2, tall, wide), BF)] * 4,
        scratch_shapes=[pltpu.VMEM((2, tall, wide), BF)] * 4
        + [pltpu.SemaphoreType.DMA((2, 4))],
        compiler_params=pltpu.CompilerParams(vmem_limit_bytes=VMEM),
        name="halves",
    )(*blocks)


def shards(grad_out, route_weights, routes, saved_gate_up, down_weight):
    n_outer = lax.axis_size("outer")
    cap = saved_gate_up.shape[3]
    hid = down_weight.shape[1]
    split = hid - WAVE_TILES * TILE
    inner, outer = lax.axis_index("inner"), lax.axis_index("outer")
    z, y, x, core = inner // 4, inner % 4, outer // 2, outer % 2
    steps = jnp.array([0, -1, 1, 2], jnp.int32)

    gathered = lax.all_gather(down_weight[:, :split], "inner", axis=0, tiled=False)

    a, b = down_weight[0, split:], down_weight[1, split:]
    pair = jnp.stack([grad_out, other_core(grad_out)])
    pair, (a, b) = lax.optimization_barrier((pair, (a, b)))
    one = [along(a, "y", 1), along(a, "y", -1), along(b, "z", 1), along(b, "z", -1)]
    near = along_x(pair)
    one, (near,) = together(one, [near])
    cut = a.shape[0] // 2
    two = [
        along(one[0][:cut], "y", 1), along(one[1][cut:], "y", -1),
        along(one[2][:cut], "z", 1), along(one[3][cut:], "z", -1),
    ]
    far = along_x(near[0])
    two, (far, named, scales) = together(two, [far, routes.T, route_weights.T])
    near_other = other_core(near)
    block_a = jnp.stack([a, one[0], one[1], jnp.concatenate(two[:2])])
    block_b = jnp.stack([b, one[2], one[3], jnp.concatenate(two[2:])])
    three = [
        along(block_a, "z", 1), along(block_a, "z", -1), along(block_b, "y", 1), along(block_b, "y", -1)
    ]

    far_other = other_core(far)
    plans = lax.all_to_all(
        plan(named, scales, n_outer), "outer", split_axis=0, concat_axis=0, tiled=True
    )
    came, went = (x + 2 * core - 1) % 4, (x + 1 - 2 * core) % 4
    opposite = (x + 2) % 4
    source = jnp.stack(
        [
            2 * x + core, 2 * x + 1 - core, 2 * came + core, 2 * came + 1 - core,
            2 * went + 1 - core, 2 * went + core, 2 * opposite + core, 2 * opposite + 1 - core,
        ]
    )
    filled = fill(source, [pair, near, near_other, far[None], far_other[None]], plans, cap)
    rows = filled[0].reshape(2, n_outer * cap, grad_out.shape[1])
    weights = filled[1].reshape(2, n_outer * cap, 128)
    out, sums = whole(rows, gathered, saved_gate_up, weights)

    three, (out, sums) = together(three, [out, sums])
    parts = halves(three)
    four = [
        along(parts[0], "z", 1), along(parts[1], "z", -1),
        along(parts[2], "y", 1), along(parts[3], "y", -1),
    ]
    (four,) = together(four)

    near_z, near_y = (z + steps) % 4, (y + steps) % 4
    order = jnp.concatenate(
        [
            (near_z[:, None] * 4 + near_y[None, :]).reshape(-1),
            (near_y[:, None] + near_z[None, :] * 4).reshape(-1),
        ]
    )
    partial = most(order, rows, [block_a, three[0], three[1], block_b, three[2], three[3]])
    out, grads = last(order, rows, four, saved_gate_up, weights, partial, sums, plans, out)
    returned = lax.all_to_all(grads, "outer", split_axis=0, concat_axis=0, tiled=True)
    return (out, pick(routes.T, returned).T)


def solution(mesh):
    in_specs = (
        P(("outer", "inner"), None),
        P(("outer", "inner"), None),
        P(("outer", "inner"), None),
        P(None, "outer", "inner", None, None),
        P("outer", None, "inner"),
    )
    out_specs = (P(None, "outer", "inner", None, None), P(("outer", "inner"), None))
    return jax.shard_map(shards, mesh=mesh, in_specs=in_specs, out_specs=out_specs, check_vma=False)
```

```python
import functools

import jax
import jax.numpy as jnp
from jax import lax
from jax.experimental import pallas as pl
from jax.experimental.pallas import tpu as pltpu
from jax.sharding import PartitionSpec as P

BF = jnp.bfloat16
F32 = jnp.float32
PARTS = 2
SHARD = 256
TILE = 512
WAVE_TILES = 2
VMEM = 56 * 1024 * 1024
MOST_VMEM = 32 * 1024 * 1024
LAST_VMEM = 50 * 1024 * 1024


def ring(axis, step):
    pairs = []
    for z in range(4):
        for y in range(4):
            if axis == "y":
                pairs.append((z * 4 + y, z * 4 + (y + step) % 4))
            else:
                pairs.append((z * 4 + y, ((z + step) % 4) * 4 + y))
    return pairs


def along(x, axis, step):
    return lax.ppermute(x, "inner", ring(axis, step))


def along_x(x):
    pairs = [(a * 2 + c, ((a + 1 - 2 * c) % 4) * 2 + c) for a in range(4) for c in range(2)]
    return lax.ppermute(x, "outer", pairs)


def other_core(x):
    return lax.ppermute(x, "outer", [(i, i ^ 1) for i in range(8)])


def together(*groups):
    return [list(g) for g in lax.optimization_barrier(tuple(tuple(g) for g in groups))]


def params(steps, vmem=VMEM):
    return pltpu.CompilerParams(
        dimension_semantics=("arbitrary",) * steps, vmem_limit_bytes=vmem
    )


def plan_kernel(routes_ref, weights_ref, out_ref):
    routes = routes_ref[...]
    weights = weights_ref[...].astype(F32)
    tokens = routes.shape[1]
    experts = out_ref.shape[0] * 2
    expert = lax.broadcasted_iota(jnp.int32, (experts, tokens), 0)
    named = jnp.zeros((experts, tokens), F32)
    weight = jnp.zeros((experts, tokens), F32)
    for k in range(routes.shape[0]):
        same = routes[k : k + 1, :] == expert
        named = jnp.where(same, 1.0, named)
        weight = jnp.where(same, weights[k : k + 1, :], weight)
    earlier = lax.broadcasted_iota(jnp.int32, (tokens, tokens), 0)
    later = lax.broadcasted_iota(jnp.int32, (tokens, tokens), 1)
    before = jnp.where(earlier < later, 1.0, 0.0).astype(BF)
    position = jnp.dot(named.astype(BF), before, preferred_element_type=F32)
    position = jnp.where(named > 0.0, position, -1.0)
    for e in range(experts):
        out_ref[e // 2, e % 2 : e % 2 + 1, :] = position[e : e + 1, :]
        out_ref[e // 2, 2 + e % 2 : 3 + e % 2, :] = weight[e : e + 1, :]


def plan(routes, route_weights, n_outer):
    return pl.pallas_call(
        plan_kernel,
        out_shape=jax.ShapeDtypeStruct((n_outer, 4, routes.shape[1]), F32),
        name="plan",
    )(routes, route_weights)


def pick_kernel(routes_ref, grads_ref, out_ref):
    routes = routes_ref[...]
    total = jnp.zeros(routes.shape, F32)
    for o in range(grads_ref.shape[0]):
        for j in range(2):
            total = jnp.where(routes == 2 * o + j, grads_ref[o, j : j + 1, :], total)
    out_ref[...] = total


def pick(routes, grads):
    return pl.pallas_call(
        pick_kernel, out_shape=jax.ShapeDtypeStruct(routes.shape, F32), name="pick"
    )(routes, grads)


def fill_block(tokens_ref, plan_ref, rows_ref, weight_ref):
    tokens = plan_ref.shape[-1]
    cap = rows_ref.shape[2]
    slot = lax.broadcasted_iota(jnp.int32, (cap, tokens), 0).astype(F32)
    width = tokens_ref.shape[-1]
    step = 1024
    picks = []
    for j in range(2):
        owned = slot == plan_ref[0, j : j + 1, :]
        picks.append(jnp.where(owned, 1.0, 0.0))
        weight = jnp.sum(
            jnp.where(owned, plan_ref[0, 2 + j : 3 + j, :], 0.0), axis=1, keepdims=True
        )
        weight_ref[j, 0] = jnp.broadcast_to(weight, weight_ref.shape[2:])
    picks = jnp.concatenate(picks, axis=0).astype(BF)
    for c in range(0, width, step):
        rows = jnp.dot(picks, tokens_ref[0, :, c : c + step], preferred_element_type=F32)
        rows_ref[0, 0, :, c : c + step] = rows[:cap].astype(BF)
        rows_ref[1, 0, :, c : c + step] = rows[cap:].astype(BF)


def fill_kernel(starts, source_ref, *refs):
    tokens_refs, (plan_ref, rows_ref, weight_ref) = refs[:-3], refs[-3:]
    q = pl.program_id(0)
    for n, tokens_ref in enumerate(tokens_refs):

        @pl.when((q >= starts[n]) & (q < starts[n + 1]))
        def _(tokens_ref=tokens_ref):
            fill_block(tokens_ref, plan_ref, rows_ref, weight_ref)


def fill(sources, tokens, plans, cap):
    _, rows, width = tokens[0].shape
    starts = [0]
    for part in tokens:
        starts.append(starts[-1] + part.shape[0])
    count = starts[-1]
    return pl.pallas_call(
        functools.partial(fill_kernel, starts),
        grid_spec=pltpu.PrefetchScalarGridSpec(
            num_scalar_prefetch=1,
            grid=(count,),
            in_specs=[
                pl.BlockSpec(
                    (1, rows, width),
                    lambda q, src, lo=starts[n], top=part.shape[0] - 1: (
                        jnp.clip(q - lo, 0, top), 0, 0
                    ),
                )
                for n, part in enumerate(tokens)
            ]
            + [pl.BlockSpec((1, 4, rows), lambda q, src: (src[q], 0, 0))],
            out_specs=[
                pl.BlockSpec((2, 1, cap, width), lambda q, src: (0, src[q], 0, 0)),
                pl.BlockSpec((2, 1, cap, 128), lambda q, src: (0, src[q], 0, 0)),
            ],
        ),
        out_shape=[
            jax.ShapeDtypeStruct((2, count, cap, width), BF),
            jax.ShapeDtypeStruct((2, count, cap, 128), F32),
        ],
        compiler_params=params(1),
        cost_estimate=pl.CostEstimate(
            flops=2 * count * 2 * cap * rows * width,
            bytes_accessed=count * (rows + 2 * cap) * width * 2,
            transcendentals=0,
        ),
        name="fill",
    )(sources, *tokens, plans)


def product(rows, weight):
    return lax.dot_general(
        rows, weight, (((1,), (1,)), ((), ())), preferred_element_type=F32
    )


def backward(total_ref, gate_ref, up_ref, weight_ref, out_ref, sums_ref, sources):
    cap = gate_ref.shape[3]
    for s in sources:
        at = slice(s * cap, (s + 1) * cap)
        weight = weight_ref[0, at, :]
        for c in range(0, TILE, 128):
            cols = slice(c, c + 128)
            carried = total_ref[at, cols]
            gate = gate_ref[s, 0, 0, :, cols].astype(F32)
            upper = up_ref[s, 0, 0, :, cols].astype(F32)
            sigma = 0.5 * jnp.tanh(0.5 * gate) + 0.5
            active = gate * sigma
            hidden = (active * upper).astype(BF).astype(F32)
            part = carried * hidden
            sums = part if c == 0 else sums + part
            scaled = weight * carried
            out_ref[0, s, :, cols] = (
                scaled * upper * (sigma + active * (1.0 - sigma))
            ).astype(BF)
            out_ref[1, s, :, cols] = (scaled * active).astype(BF)
        sums_ref[at, :] += sums


def out_copies(stage_ref, out_ref, sems, slot, j, tile):
    hid = out_ref.shape[-1] // 2
    return [
        pltpu.make_async_copy(
            stage_ref.at[slot, half],
            out_ref.at[:, j, 0, :, pl.ds(pl.multiple_of(half * hid + tile * TILE, TILE), TILE)],
            sems.at[slot, half],
        )
        for half in range(2)
    ]


def staged(stage_ref, out_ref, sems, j, tile, tiles, first, compute):
    step = j * tiles + tile
    slot = step % 2

    @pl.when(step >= 2)
    def _():
        old = step - 2
        for copy in out_copies(
            stage_ref, out_ref, sems, slot, old // tiles, first + old % tiles
        ):
            copy.wait()

    compute(stage_ref.at[slot])
    for copy in out_copies(stage_ref, out_ref, sems, slot, j, first + tile):
        copy.start()

    @pl.when(step == 2 * tiles - 1)
    def _():
        old = step - 1
        for copy in out_copies(
            stage_ref, out_ref, sems, 1 - slot, old // tiles, first + old % tiles
        ):
            copy.wait()
        for copy in out_copies(stage_ref, out_ref, sems, slot, j, first + tile):
            copy.wait()


QUARTER = 1024


def row_copies(rows_ref, held_ref, sems, j):
    return [
        (
            rows_ref.at[j, :, pl.ds(k * QUARTER, QUARTER)],
            held_ref.at[j, :, pl.ds(k * QUARTER, QUARTER)],
            sems.at[j, k],
        )
        for k in range(held_ref.shape[2] // QUARTER)
    ]


def start_rows(rows_ref, held_ref, sems):
    for e in range(2):
        for copy in row_copies(rows_ref, held_ref, sems, e):
            pltpu.make_async_copy(*copy).start()


def whole_kernel(tiles, rows_ref, w_ref, gate_ref, up_ref, weight_ref, *rest):
    out_ref, sums_ref, total_ref, stage_ref, out_sems, held_ref, sems = rest
    j, tile = pl.program_id(0), pl.program_id(1)

    @pl.when((j == 0) & (tile == 0))
    def _():
        start_rows(rows_ref, held_ref, sems)

    @pl.when(tile == 0)
    def _():
        sums_ref[...] = jnp.zeros_like(sums_ref)

    for k in range(4):

        @pl.when(tile == 0)
        def _(k=k):
            pltpu.make_async_copy(*row_copies(rows_ref, held_ref, sems, j)[k]).wait()

        weight = jnp.concatenate([w_ref[4 * k + i, 0] for i in range(4)], axis=1)
        part = product(held_ref[j, :, k * QUARTER : (k + 1) * QUARTER], weight)
        total_ref[...] = part if k == 0 else total_ref[...] + part

    def compute(slot_ref):
        backward(
            total_ref, gate_ref, up_ref, weight_ref, slot_ref, sums_ref.at[0],
            range(gate_ref.shape[0]),
        )

    staged(stage_ref, out_ref, out_sems, j, tile, tiles, 0, compute)


def whole(rows, w, saved, weights):
    _, slots, width = rows.shape
    sources, _, _, cap, both = saved.shape
    tiles = w.shape[2] // TILE
    shift = both // 2 // TILE
    tile = (sources, 1, 1, cap, TILE)
    return pl.pallas_call(
        functools.partial(whole_kernel, tiles),
        grid=(2, tiles),
        in_specs=[
            pl.BlockSpec(memory_space=pl.ANY),
            pl.BlockSpec((16, 1, TILE, SHARD), lambda j, h: (0, j, h, 0)),
            pl.BlockSpec(tile, lambda j, h: (0, j, 0, 0, h)),
            pl.BlockSpec(tile, lambda j, h: (0, j, 0, 0, h + shift)),
            pl.BlockSpec((1, slots, 128), lambda j, h: (j, 0, 0)),
        ],
        out_specs=[
            pl.BlockSpec(memory_space=pl.ANY),
            pl.BlockSpec((1, slots, 128), lambda j, h: (j, 0, 0)),
        ],
        out_shape=[
            jax.ShapeDtypeStruct(saved.shape, BF),
            jax.ShapeDtypeStruct((2, slots, 128), F32),
        ],
        scratch_shapes=[
            pltpu.VMEM((slots, TILE), F32),
            pltpu.VMEM((2, 2, sources, cap, TILE), BF),
            pltpu.SemaphoreType.DMA((2, 2)),
            pltpu.VMEM(rows.shape, BF),
            pltpu.SemaphoreType.DMA((2, width // QUARTER)),
        ],
        compiler_params=params(2),
        cost_estimate=pl.CostEstimate(
            flops=4 * slots * width * tiles * TILE,
            bytes_accessed=4 * slots * width + 4 * tiles * TILE * (width + 4 * slots),
            transcendentals=2 * slots * tiles * TILE,
        ),
        name="whole",
    )(rows, w, saved, saved, weights)


def columns(ref, j, order_ref, first):
    return jnp.concatenate(
        [
            ref[j, :, pl.ds(pl.multiple_of(order_ref[first + i] * SHARD, SHARD), SHARD)]
            for i in range(4)
        ],
        axis=1,
    )


def most_kernel(order_ref, rows_ref, *rest):
    blocks, (total_ref, held_ref, sems) = rest[:6], rest[6:]
    j, tile = pl.program_id(0), pl.program_id(1)

    @pl.when((j == 0) & (tile == 0))
    def _():
        start_rows(rows_ref, held_ref, sems)

    @pl.when(tile == 0)
    def _():
        for copy in row_copies(rows_ref, held_ref, sems, j):
            pltpu.make_async_copy(*copy).wait()

    for e in range(2):

        @pl.when(j == e)
        def _(e=e):
            for n, w_ref in enumerate(blocks[3 * e : 3 * e + 3]):
                weight = jnp.concatenate([w_ref[i] for i in range(4)], axis=1)
                part = product(columns(held_ref, e, order_ref, 16 * e + 4 * n), weight)
                total_ref[0] = part if n == 0 else total_ref[0] + part


def a_map(tiles, j, h, o):
    return 0, jnp.where(j == 0, h, tiles - 1), 0


def b_map(j, h, o):
    return 0, jnp.where(j == 0, 0, h), 0


def most(order, rows, blocks):
    _, slots, width = rows.shape
    tiles = blocks[0].shape[1] // TILE
    return pl.pallas_call(
        most_kernel,
        grid_spec=pltpu.PrefetchScalarGridSpec(
            num_scalar_prefetch=1,
            grid=(2, tiles),
            in_specs=[pl.BlockSpec(memory_space=pl.ANY)]
            + [pl.BlockSpec((4, TILE, SHARD), functools.partial(a_map, tiles))] * 3
            + [pl.BlockSpec((4, TILE, SHARD), b_map)] * 3,
            out_specs=pl.BlockSpec((1, slots, TILE), lambda j, h, o: (j, 0, h)),
            scratch_shapes=[
                pltpu.VMEM(rows.shape, BF),
                pltpu.SemaphoreType.DMA((2, width // QUARTER)),
            ],
        ),
        out_shape=jax.ShapeDtypeStruct((2, slots, tiles * TILE), F32),
        compiler_params=params(2, MOST_VMEM),
        cost_estimate=pl.CostEstimate(
            flops=4 * slots * width * tiles * TILE * 3 // 4,
            bytes_accessed=4 * slots * width + 2 * tiles * TILE * (2 * width + 4 * slots),
            transcendentals=0,
        ),
        name="most",
    )(order, rows, *blocks)


def last_kernel(first, tiles, order_ref, *rest):
    columns_refs, blocks = rest[:4], rest[4:8]
    gate_ref, up_ref, weight_ref, most_ref, before_ref, plan_ref = rest[8:14]
    out_ref, grads_ref, total_ref, stage_ref, out_sems, sums_ref = rest[15:]
    j, tile = pl.program_id(0), pl.program_id(1)

    @pl.when(tile == 0)
    def _():
        sums_ref[...] = before_ref[0]

    sources, cap = gate_ref.shape[0], gate_ref.shape[3]
    group = sources // PARTS

    def compute(slot_ref):
        for e in range(2):

            @pl.when(j == e)
            def _(e=e):
                a_ref, b_ref = blocks[2 * e : 2 * e + 2]
                weight = jnp.concatenate([a_ref[0], a_ref[1], b_ref[0], b_ref[1]], axis=1)

                def multiply(n):
                    at = slice(n * group * cap, (n + 1) * group * cap)
                    rows = jnp.concatenate([ref[0, at, :] for ref in columns_refs], axis=1)
                    total_ref[at, :] = most_ref[0, at, :] + product(rows, weight)

                multiply(0)
                for n in range(PARTS):
                    if n + 1 < PARTS:
                        multiply(n + 1)
                    backward(
                        total_ref, gate_ref, up_ref, weight_ref, slot_ref, sums_ref,
                        range(n * group, (n + 1) * group),
                    )

    staged(stage_ref, out_ref, out_sems, j, tile, tiles, first, compute)

    @pl.when(tile == tiles - 1)
    def _():
        cap, tokens = gate_ref.shape[3], plan_ref.shape[-1]
        slot = lax.broadcasted_iota(jnp.int32, (cap, tokens), 0).astype(F32)
        for s in range(gate_ref.shape[0]):
            value = jnp.sum(sums_ref[s * cap : (s + 1) * cap, :], axis=1, keepdims=True)
            owned = slot == plan_ref[s, pl.ds(j, 1), :]
            grads_ref[s, pl.ds(j, 1), :] = jnp.sum(
                jnp.where(owned, value, 0.0), axis=0, keepdims=True
            )


def last(order, rows, blocks, saved, weights, partial, before, plans, out):
    _, slots, width = rows.shape
    sources, _, _, cap, both = saved.shape
    tiles = blocks[0].shape[1] // TILE
    shift = both // 2 // TILE
    first = shift - tiles
    tokens = plans.shape[-1]
    tile = (sources, 1, 1, cap, TILE)
    return pl.pallas_call(
        functools.partial(last_kernel, first, tiles),
        grid_spec=pltpu.PrefetchScalarGridSpec(
            num_scalar_prefetch=1,
            grid=(2, tiles),
            in_specs=[
                pl.BlockSpec(
                    (1, slots, SHARD), lambda j, h, o, i=i: (j, 0, o[16 * j + 12 + i])
                )
                for i in range(4)
            ]
            + [pl.BlockSpec((2, TILE, SHARD), functools.partial(a_map, tiles))] * 2
            + [pl.BlockSpec((2, TILE, SHARD), b_map)] * 2
            + [
                pl.BlockSpec(tile, lambda j, h, o: (0, j, 0, 0, first + h)),
                pl.BlockSpec(tile, lambda j, h, o: (0, j, 0, 0, first + h + shift)),
                pl.BlockSpec((1, slots, 128), lambda j, h, o: (j, 0, 0)),
                pl.BlockSpec((1, slots, TILE), lambda j, h, o: (j, 0, h)),
                pl.BlockSpec((1, slots, 128), lambda j, h, o: (j, 0, 0)),
                pl.BlockSpec((sources, 4, tokens), lambda j, h, o: (0, 0, 0)),
                pl.BlockSpec(memory_space=pl.ANY),
            ],
            out_specs=[
                pl.BlockSpec(memory_space=pl.ANY),
                pl.BlockSpec((sources, 2, tokens), lambda j, h, o: (0, 0, 0)),
            ],
            scratch_shapes=[
                pltpu.VMEM((slots, TILE), F32),
                pltpu.VMEM((2, 2, sources, cap, TILE), BF),
                pltpu.SemaphoreType.DMA((2, 2)),
                pltpu.VMEM((slots, 128), F32),
            ],
        ),
        out_shape=[
            jax.ShapeDtypeStruct(saved.shape, BF),
            jax.ShapeDtypeStruct((sources, 2, tokens), F32),
        ],
        input_output_aliases={15: 0},
        compiler_params=params(2, LAST_VMEM),
        cost_estimate=pl.CostEstimate(
            flops=4 * slots * width * tiles * TILE // 4,
            bytes_accessed=2 * slots * width + 2 * tiles * TILE * (width + 12 * slots),
            transcendentals=2 * slots * tiles * TILE,
        ),
        name="last",
    )(
        order, rows, rows, rows, rows, *blocks, saved, saved, weights, partial, before,
        plans, out,
    )


def halves_kernel(*refs):
    blocks, parts, held, sems = refs[:4], refs[4:8], refs[8:12], refs[12]
    reads = [
        pltpu.make_async_copy(blocks[n].at[pl.ds(2 * (n % 2), 2)], held[n], sems.at[0, n])
        for n in range(4)
    ]
    writes = [pltpu.make_async_copy(held[n], parts[n], sems.at[1, n]) for n in range(4)]
    for copy in reads:
        copy.start()
    for read, write in zip(reads, writes):
        read.wait()
        write.start()
    for copy in writes:
        copy.wait()


def halves(blocks):
    _, tall, wide = blocks[0].shape
    return pl.pallas_call(
        halves_kernel,
        in_specs=[pl.BlockSpec(memory_space=pl.ANY)] * 4,
        out_specs=[pl.BlockSpec(memory_space=pl.ANY)] * 4,
        out_shape=[jax.ShapeDtypeStruct((2, tall, wide), BF)] * 4,
        scratch_shapes=[pltpu.VMEM((2, tall, wide), BF)] * 4
        + [pltpu.SemaphoreType.DMA((2, 4))],
        compiler_params=pltpu.CompilerParams(vmem_limit_bytes=VMEM),
        name="halves",
    )(*blocks)


def shards(grad_out, route_weights, routes, saved_gate_up, down_weight):
    n_outer = lax.axis_size("outer")
    cap = saved_gate_up.shape[3]
    hid = down_weight.shape[1]
    split = hid - WAVE_TILES * TILE
    inner, outer = lax.axis_index("inner"), lax.axis_index("outer")
    z, y, x, core = inner // 4, inner % 4, outer // 2, outer % 2
    steps = jnp.array([0, -1, 1, 2], jnp.int32)

    gathered = lax.all_gather(down_weight[:, :split], "inner", axis=0, tiled=False)

    a, b = down_weight[0, split:], down_weight[1, split:]
    one = [along(a, "y", 1), along(a, "y", -1), along(b, "z", 1), along(b, "z", -1)]
    one, (next_one,) = together(one, [along_x(grad_out)])
    cut = a.shape[0] // 2
    two = [
        along(one[0][:cut], "y", 1), along(one[1][cut:], "y", -1),
        along(one[2][:cut], "z", 1), along(one[3][cut:], "z", -1),
    ]
    two, (next_two, named, scales) = together(
        two, [along_x(next_one), routes.T, route_weights.T]
    )
    block_a = jnp.stack([a, one[0], one[1], jnp.concatenate(two[:2])])
    block_b = jnp.stack([b, one[2], one[3], jnp.concatenate(two[2:])])
    three = [
        along(block_a, "z", 1), along(block_a, "z", -1), along(block_b, "y", 1), along(block_b, "y", -1)
    ]

    near = jnp.stack([grad_out, next_one, next_two])
    last_one = along_x(next_two)[None]
    near_other, last_other = other_core(near), other_core(last_one)
    plans = lax.all_to_all(
        plan(named, scales, n_outer), "outer", split_axis=0, concat_axis=0, tiled=True
    )
    back = 2 * core - 1
    source = jnp.stack(
        [((x + n * back) % 4) * 2 + core for n in range(4)]
        + [((x - n * back) % 4) * 2 + 1 - core for n in range(4)]
    )
    filled = fill(source, [near, last_one, near_other, last_other], plans, cap)
    rows = filled[0].reshape(2, n_outer * cap, grad_out.shape[1])
    weights = filled[1].reshape(2, n_outer * cap, 128)
    out, sums = whole(rows, gathered, saved_gate_up, weights)

    three, (out, sums) = together(three, [out, sums])
    parts = halves(three)
    four = [
        along(parts[0], "z", 1), along(parts[1], "z", -1),
        along(parts[2], "y", 1), along(parts[3], "y", -1),
    ]
    (four,) = together(four)

    near_z, near_y = (z + steps) % 4, (y + steps) % 4
    order = jnp.concatenate(
        [
            (near_z[:, None] * 4 + near_y[None, :]).reshape(-1),
            (near_y[:, None] + near_z[None, :] * 4).reshape(-1),
        ]
    )
    partial = most(order, rows, [block_a, three[0], three[1], block_b, three[2], three[3]])
    out, grads = last(order, rows, four, saved_gate_up, weights, partial, sums, plans, out)
    returned = lax.all_to_all(grads, "outer", split_axis=0, concat_axis=0, tiled=True)
    return (out, pick(routes.T, returned).T)


def solution(mesh):
    in_specs = (
        P(("outer", "inner"), None),
        P(("outer", "inner"), None),
        P(("outer", "inner"), None),
        P(None, "outer", "inner", None, None),
        P("outer", None, "inner"),
    )
    out_specs = (P(None, "outer", "inner", None, None), P(("outer", "inner"), None))
    return jax.shard_map(shards, mesh=mesh, in_specs=in_specs, out_specs=out_specs, check_vma=False)
```

```python
import functools

import jax
import jax.numpy as jnp
from jax import lax
from jax.experimental import pallas as pl
from jax.experimental.pallas import tpu as pltpu
from jax.sharding import PartitionSpec as P

BF = jnp.bfloat16
F32 = jnp.float32
PARTS = 2
SHARD = 256
TILE = 512
WAVE_TILES = 2
VMEM = 56 * 1024 * 1024
MOST_VMEM = 32 * 1024 * 1024
LAST_VMEM = 50 * 1024 * 1024


def ring(axis, step):
    pairs = []
    for z in range(4):
        for y in range(4):
            if axis == "y":
                pairs.append((z * 4 + y, z * 4 + (y + step) % 4))
            else:
                pairs.append((z * 4 + y, ((z + step) % 4) * 4 + y))
    return pairs


def along(x, axis, step):
    return lax.ppermute(x, "inner", ring(axis, step))


def along_x(x, way=1):
    pairs = [
        (a * 2 + c, ((a + way * (1 - 2 * c)) % 4) * 2 + c) for a in range(4) for c in range(2)
    ]
    return lax.ppermute(x, "outer", pairs)


def other_core(x):
    return lax.ppermute(x, "outer", [(i, i ^ 1) for i in range(8)])


def together(*groups):
    return [list(g) for g in lax.optimization_barrier(tuple(tuple(g) for g in groups))]


def params(steps, vmem=VMEM):
    return pltpu.CompilerParams(
        dimension_semantics=("arbitrary",) * steps, vmem_limit_bytes=vmem
    )


def plan_kernel(routes_ref, weights_ref, out_ref):
    routes = routes_ref[...]
    weights = weights_ref[...].astype(F32)
    tokens = routes.shape[1]
    experts = out_ref.shape[0] * 2
    expert = lax.broadcasted_iota(jnp.int32, (experts, tokens), 0)
    named = jnp.zeros((experts, tokens), F32)
    weight = jnp.zeros((experts, tokens), F32)
    for k in range(routes.shape[0]):
        same = routes[k : k + 1, :] == expert
        named = jnp.where(same, 1.0, named)
        weight = jnp.where(same, weights[k : k + 1, :], weight)
    earlier = lax.broadcasted_iota(jnp.int32, (tokens, tokens), 0)
    later = lax.broadcasted_iota(jnp.int32, (tokens, tokens), 1)
    before = jnp.where(earlier < later, 1.0, 0.0).astype(BF)
    position = jnp.dot(named.astype(BF), before, preferred_element_type=F32)
    position = jnp.where(named > 0.0, position, -1.0)
    for e in range(experts):
        out_ref[e // 2, e % 2 : e % 2 + 1, :] = position[e : e + 1, :]
        out_ref[e // 2, 2 + e % 2 : 3 + e % 2, :] = weight[e : e + 1, :]


def plan(routes, route_weights, n_outer):
    return pl.pallas_call(
        plan_kernel,
        out_shape=jax.ShapeDtypeStruct((n_outer, 4, routes.shape[1]), F32),
        name="plan",
    )(routes, route_weights)


def pick_kernel(routes_ref, grads_ref, out_ref):
    routes = routes_ref[...]
    total = jnp.zeros(routes.shape, F32)
    for o in range(grads_ref.shape[0]):
        for j in range(2):
            total = jnp.where(routes == 2 * o + j, grads_ref[o, j : j + 1, :], total)
    out_ref[...] = total


def pick(routes, grads):
    return pl.pallas_call(
        pick_kernel, out_shape=jax.ShapeDtypeStruct(routes.shape, F32), name="pick"
    )(routes, grads)


def fill_block(tokens_ref, plan_ref, rows_ref, weight_ref):
    tokens = plan_ref.shape[-1]
    cap = rows_ref.shape[2]
    slot = lax.broadcasted_iota(jnp.int32, (cap, tokens), 0).astype(F32)
    width = tokens_ref.shape[-1]
    step = 1024
    picks = []
    for j in range(2):
        owned = slot == plan_ref[0, j : j + 1, :]
        picks.append(jnp.where(owned, 1.0, 0.0))
        weight = jnp.sum(
            jnp.where(owned, plan_ref[0, 2 + j : 3 + j, :], 0.0), axis=1, keepdims=True
        )
        weight_ref[j, 0] = jnp.broadcast_to(weight, weight_ref.shape[2:])
    picks = jnp.concatenate(picks, axis=0).astype(BF)
    for c in range(0, width, step):
        rows = jnp.dot(picks, tokens_ref[0, :, c : c + step], preferred_element_type=F32)
        rows_ref[0, 0, :, c : c + step] = rows[:cap].astype(BF)
        rows_ref[1, 0, :, c : c + step] = rows[cap:].astype(BF)


def fill_kernel(starts, source_ref, *refs):
    tokens_refs, (plan_ref, rows_ref, weight_ref) = refs[:-3], refs[-3:]
    q = pl.program_id(0)
    for n, tokens_ref in enumerate(tokens_refs):

        @pl.when((q >= starts[n]) & (q < starts[n + 1]))
        def _(tokens_ref=tokens_ref):
            fill_block(tokens_ref, plan_ref, rows_ref, weight_ref)


def fill(sources, tokens, plans, cap):
    _, rows, width = tokens[0].shape
    starts = [0]
    for part in tokens:
        starts.append(starts[-1] + part.shape[0])
    count = starts[-1]
    return pl.pallas_call(
        functools.partial(fill_kernel, starts),
        grid_spec=pltpu.PrefetchScalarGridSpec(
            num_scalar_prefetch=1,
            grid=(count,),
            in_specs=[
                pl.BlockSpec(
                    (1, rows, width),
                    lambda q, src, lo=starts[n], top=part.shape[0] - 1: (
                        jnp.clip(q - lo, 0, top), 0, 0
                    ),
                )
                for n, part in enumerate(tokens)
            ]
            + [pl.BlockSpec((1, 4, rows), lambda q, src: (src[q], 0, 0))],
            out_specs=[
                pl.BlockSpec((2, 1, cap, width), lambda q, src: (0, src[q], 0, 0)),
                pl.BlockSpec((2, 1, cap, 128), lambda q, src: (0, src[q], 0, 0)),
            ],
        ),
        out_shape=[
            jax.ShapeDtypeStruct((2, count, cap, width), BF),
            jax.ShapeDtypeStruct((2, count, cap, 128), F32),
        ],
        compiler_params=params(1),
        cost_estimate=pl.CostEstimate(
            flops=2 * count * 2 * cap * rows * width,
            bytes_accessed=count * (rows + 2 * cap) * width * 2,
            transcendentals=0,
        ),
        name="fill",
    )(sources, *tokens, plans)


def product(rows, weight):
    return lax.dot_general(
        rows, weight, (((1,), (1,)), ((), ())), preferred_element_type=F32
    )


def backward(total_ref, gate_ref, up_ref, weight_ref, out_ref, sums_ref, sources):
    cap = gate_ref.shape[3]
    for s in sources:
        at = slice(s * cap, (s + 1) * cap)
        weight = weight_ref[0, at, :]
        for c in range(0, TILE, 128):
            cols = slice(c, c + 128)
            carried = total_ref[at, cols]
            gate = gate_ref[s, 0, 0, :, cols].astype(F32)
            upper = up_ref[s, 0, 0, :, cols].astype(F32)
            sigma = 0.5 * jnp.tanh(0.5 * gate) + 0.5
            active = gate * sigma
            hidden = (active * upper).astype(BF).astype(F32)
            part = carried * hidden
            sums = part if c == 0 else sums + part
            scaled = weight * carried
            out_ref[0, s, :, cols] = (
                scaled * upper * (sigma + active * (1.0 - sigma))
            ).astype(BF)
            out_ref[1, s, :, cols] = (scaled * active).astype(BF)
        sums_ref[at, :] += sums


def out_copies(stage_ref, out_ref, sems, slot, j, tile):
    hid = out_ref.shape[-1] // 2
    return [
        pltpu.make_async_copy(
            stage_ref.at[slot, half],
            out_ref.at[:, j, 0, :, pl.ds(pl.multiple_of(half * hid + tile * TILE, TILE), TILE)],
            sems.at[slot, half],
        )
        for half in range(2)
    ]


def staged(stage_ref, out_ref, sems, j, tile, tiles, first, compute):
    step = j * tiles + tile
    slot = step % 2

    @pl.when(step >= 2)
    def _():
        old = step - 2
        for copy in out_copies(
            stage_ref, out_ref, sems, slot, old // tiles, first + old % tiles
        ):
            copy.wait()

    compute(stage_ref.at[slot])
    for copy in out_copies(stage_ref, out_ref, sems, slot, j, first + tile):
        copy.start()

    @pl.when(step == 2 * tiles - 1)
    def _():
        old = step - 1
        for copy in out_copies(
            stage_ref, out_ref, sems, 1 - slot, old // tiles, first + old % tiles
        ):
            copy.wait()
        for copy in out_copies(stage_ref, out_ref, sems, slot, j, first + tile):
            copy.wait()


QUARTER = 1024


def row_copies(rows_ref, held_ref, sems, j):
    return [
        (
            rows_ref.at[j, :, pl.ds(k * QUARTER, QUARTER)],
            held_ref.at[j, :, pl.ds(k * QUARTER, QUARTER)],
            sems.at[j, k],
        )
        for k in range(held_ref.shape[2] // QUARTER)
    ]


def start_rows(rows_ref, held_ref, sems):
    for e in range(2):
        for copy in row_copies(rows_ref, held_ref, sems, e):
            pltpu.make_async_copy(*copy).start()


def whole_kernel(tiles, rows_ref, w_ref, gate_ref, up_ref, weight_ref, *rest):
    out_ref, sums_ref, total_ref, stage_ref, out_sems, held_ref, sems = rest
    j, tile = pl.program_id(0), pl.program_id(1)

    @pl.when((j == 0) & (tile == 0))
    def _():
        start_rows(rows_ref, held_ref, sems)

    @pl.when(tile == 0)
    def _():
        sums_ref[...] = jnp.zeros_like(sums_ref)

    for k in range(4):

        @pl.when(tile == 0)
        def _(k=k):
            pltpu.make_async_copy(*row_copies(rows_ref, held_ref, sems, j)[k]).wait()

        weight = jnp.concatenate([w_ref[4 * k + i, 0] for i in range(4)], axis=1)
        part = product(held_ref[j, :, k * QUARTER : (k + 1) * QUARTER], weight)
        total_ref[...] = part if k == 0 else total_ref[...] + part

    def compute(slot_ref):
        backward(
            total_ref, gate_ref, up_ref, weight_ref, slot_ref, sums_ref.at[0],
            range(gate_ref.shape[0]),
        )

    staged(stage_ref, out_ref, out_sems, j, tile, tiles, 0, compute)


def whole(rows, w, saved, weights):
    _, slots, width = rows.shape
    sources, _, _, cap, both = saved.shape
    tiles = w.shape[2] // TILE
    shift = both // 2 // TILE
    tile = (sources, 1, 1, cap, TILE)
    return pl.pallas_call(
        functools.partial(whole_kernel, tiles),
        grid=(2, tiles),
        in_specs=[
            pl.BlockSpec(memory_space=pl.ANY),
            pl.BlockSpec((16, 1, TILE, SHARD), lambda j, h: (0, j, h, 0)),
            pl.BlockSpec(tile, lambda j, h: (0, j, 0, 0, h)),
            pl.BlockSpec(tile, lambda j, h: (0, j, 0, 0, h + shift)),
            pl.BlockSpec((1, slots, 128), lambda j, h: (j, 0, 0)),
        ],
        out_specs=[
            pl.BlockSpec(memory_space=pl.ANY),
            pl.BlockSpec((1, slots, 128), lambda j, h: (j, 0, 0)),
        ],
        out_shape=[
            jax.ShapeDtypeStruct(saved.shape, BF),
            jax.ShapeDtypeStruct((2, slots, 128), F32),
        ],
        scratch_shapes=[
            pltpu.VMEM((slots, TILE), F32),
            pltpu.VMEM((2, 2, sources, cap, TILE), BF),
            pltpu.SemaphoreType.DMA((2, 2)),
            pltpu.VMEM(rows.shape, BF),
            pltpu.SemaphoreType.DMA((2, width // QUARTER)),
        ],
        compiler_params=params(2),
        cost_estimate=pl.CostEstimate(
            flops=4 * slots * width * tiles * TILE,
            bytes_accessed=4 * slots * width + 4 * tiles * TILE * (width + 4 * slots),
            transcendentals=2 * slots * tiles * TILE,
        ),
        name="whole",
    )(rows, w, saved, saved, weights)


def columns(ref, j, order_ref, first):
    return jnp.concatenate(
        [
            ref[j, :, pl.ds(pl.multiple_of(order_ref[first + i] * SHARD, SHARD), SHARD)]
            for i in range(4)
        ],
        axis=1,
    )


def most_kernel(order_ref, rows_ref, *rest):
    blocks, (total_ref, held_ref, sems) = rest[:6], rest[6:]
    j, tile = pl.program_id(0), pl.program_id(1)

    @pl.when((j == 0) & (tile == 0))
    def _():
        start_rows(rows_ref, held_ref, sems)

    @pl.when(tile == 0)
    def _():
        for copy in row_copies(rows_ref, held_ref, sems, j):
            pltpu.make_async_copy(*copy).wait()

    for e in range(2):

        @pl.when(j == e)
        def _(e=e):
            for n, w_ref in enumerate(blocks[3 * e : 3 * e + 3]):
                weight = jnp.concatenate([w_ref[i] for i in range(4)], axis=1)
                part = product(columns(held_ref, e, order_ref, 16 * e + 4 * n), weight)
                total_ref[0] = part if n == 0 else total_ref[0] + part


def a_map(tiles, j, h, o):
    return 0, jnp.where(j == 0, h, tiles - 1), 0


def b_map(j, h, o):
    return 0, jnp.where(j == 0, 0, h), 0


def most(order, rows, blocks):
    _, slots, width = rows.shape
    tiles = blocks[0].shape[1] // TILE
    return pl.pallas_call(
        most_kernel,
        grid_spec=pltpu.PrefetchScalarGridSpec(
            num_scalar_prefetch=1,
            grid=(2, tiles),
            in_specs=[pl.BlockSpec(memory_space=pl.ANY)]
            + [pl.BlockSpec((4, TILE, SHARD), functools.partial(a_map, tiles))] * 3
            + [pl.BlockSpec((4, TILE, SHARD), b_map)] * 3,
            out_specs=pl.BlockSpec((1, slots, TILE), lambda j, h, o: (j, 0, h)),
            scratch_shapes=[
                pltpu.VMEM(rows.shape, BF),
                pltpu.SemaphoreType.DMA((2, width // QUARTER)),
            ],
        ),
        out_shape=jax.ShapeDtypeStruct((2, slots, tiles * TILE), F32),
        compiler_params=params(2, MOST_VMEM),
        cost_estimate=pl.CostEstimate(
            flops=4 * slots * width * tiles * TILE * 3 // 4,
            bytes_accessed=4 * slots * width + 2 * tiles * TILE * (2 * width + 4 * slots),
            transcendentals=0,
        ),
        name="most",
    )(order, rows, *blocks)


def last_kernel(first, tiles, order_ref, *rest):
    columns_refs, blocks = rest[:4], rest[4:8]
    gate_ref, up_ref, weight_ref, most_ref, before_ref, plan_ref = rest[8:14]
    out_ref, grads_ref, total_ref, stage_ref, out_sems, sums_ref = rest[15:]
    j, tile = pl.program_id(0), pl.program_id(1)

    @pl.when(tile == 0)
    def _():
        sums_ref[...] = before_ref[0]

    sources, cap = gate_ref.shape[0], gate_ref.shape[3]
    group = sources // PARTS

    def compute(slot_ref):
        for e in range(2):

            @pl.when(j == e)
            def _(e=e):
                a_ref, b_ref = blocks[2 * e : 2 * e + 2]
                weight = jnp.concatenate([a_ref[0], a_ref[1], b_ref[0], b_ref[1]], axis=1)

                def multiply(n):
                    at = slice(n * group * cap, (n + 1) * group * cap)
                    rows = jnp.concatenate([ref[0, at, :] for ref in columns_refs], axis=1)
                    total_ref[at, :] = most_ref[0, at, :] + product(rows, weight)

                multiply(0)
                for n in range(PARTS):
                    if n + 1 < PARTS:
                        multiply(n + 1)
                    backward(
                        total_ref, gate_ref, up_ref, weight_ref, slot_ref, sums_ref,
                        range(n * group, (n + 1) * group),
                    )

    staged(stage_ref, out_ref, out_sems, j, tile, tiles, first, compute)

    @pl.when(tile == tiles - 1)
    def _():
        cap, tokens = gate_ref.shape[3], plan_ref.shape[-1]
        slot = lax.broadcasted_iota(jnp.int32, (cap, tokens), 0).astype(F32)
        for s in range(gate_ref.shape[0]):
            value = jnp.sum(sums_ref[s * cap : (s + 1) * cap, :], axis=1, keepdims=True)
            owned = slot == plan_ref[s, pl.ds(j, 1), :]
            grads_ref[s, pl.ds(j, 1), :] = jnp.sum(
                jnp.where(owned, value, 0.0), axis=0, keepdims=True
            )


def last(order, rows, blocks, saved, weights, partial, before, plans, out):
    _, slots, width = rows.shape
    sources, _, _, cap, both = saved.shape
    tiles = blocks[0].shape[1] // TILE
    shift = both // 2 // TILE
    first = shift - tiles
    tokens = plans.shape[-1]
    tile = (sources, 1, 1, cap, TILE)
    return pl.pallas_call(
        functools.partial(last_kernel, first, tiles),
        grid_spec=pltpu.PrefetchScalarGridSpec(
            num_scalar_prefetch=1,
            grid=(2, tiles),
            in_specs=[
                pl.BlockSpec(
                    (1, slots, SHARD), lambda j, h, o, i=i: (j, 0, o[16 * j + 12 + i])
                )
                for i in range(4)
            ]
            + [pl.BlockSpec((2, TILE, SHARD), functools.partial(a_map, tiles))] * 2
            + [pl.BlockSpec((2, TILE, SHARD), b_map)] * 2
            + [
                pl.BlockSpec(tile, lambda j, h, o: (0, j, 0, 0, first + h)),
                pl.BlockSpec(tile, lambda j, h, o: (0, j, 0, 0, first + h + shift)),
                pl.BlockSpec((1, slots, 128), lambda j, h, o: (j, 0, 0)),
                pl.BlockSpec((1, slots, TILE), lambda j, h, o: (j, 0, h)),
                pl.BlockSpec((1, slots, 128), lambda j, h, o: (j, 0, 0)),
                pl.BlockSpec((sources, 4, tokens), lambda j, h, o: (0, 0, 0)),
                pl.BlockSpec(memory_space=pl.ANY),
            ],
            out_specs=[
                pl.BlockSpec(memory_space=pl.ANY),
                pl.BlockSpec((sources, 2, tokens), lambda j, h, o: (0, 0, 0)),
            ],
            scratch_shapes=[
                pltpu.VMEM((slots, TILE), F32),
                pltpu.VMEM((2, 2, sources, cap, TILE), BF),
                pltpu.SemaphoreType.DMA((2, 2)),
                pltpu.VMEM((slots, 128), F32),
            ],
        ),
        out_shape=[
            jax.ShapeDtypeStruct(saved.shape, BF),
            jax.ShapeDtypeStruct((sources, 2, tokens), F32),
        ],
        input_output_aliases={15: 0},
        compiler_params=params(2, LAST_VMEM),
        cost_estimate=pl.CostEstimate(
            flops=4 * slots * width * tiles * TILE // 4,
            bytes_accessed=2 * slots * width + 2 * tiles * TILE * (width + 12 * slots),
            transcendentals=2 * slots * tiles * TILE,
        ),
        name="last",
    )(
        order, rows, rows, rows, rows, *blocks, saved, saved, weights, partial, before,
        plans, out,
    )


def halves_kernel(*refs):
    blocks, parts, held, sems = refs[:4], refs[4:8], refs[8:12], refs[12]
    reads = [
        pltpu.make_async_copy(blocks[n].at[pl.ds(2 * (n % 2), 2)], held[n], sems.at[0, n])
        for n in range(4)
    ]
    writes = [pltpu.make_async_copy(held[n], parts[n], sems.at[1, n]) for n in range(4)]
    for copy in reads:
        copy.start()
    for read, write in zip(reads, writes):
        read.wait()
        write.start()
    for copy in writes:
        copy.wait()


def halves(blocks):
    _, tall, wide = blocks[0].shape
    return pl.pallas_call(
        halves_kernel,
        in_specs=[pl.BlockSpec(memory_space=pl.ANY)] * 4,
        out_specs=[pl.BlockSpec(memory_space=pl.ANY)] * 4,
        out_shape=[jax.ShapeDtypeStruct((2, tall, wide), BF)] * 4,
        scratch_shapes=[pltpu.VMEM((2, tall, wide), BF)] * 4
        + [pltpu.SemaphoreType.DMA((2, 4))],
        compiler_params=pltpu.CompilerParams(vmem_limit_bytes=VMEM),
        name="halves",
    )(*blocks)


def shards(grad_out, route_weights, routes, saved_gate_up, down_weight):
    n_outer = lax.axis_size("outer")
    cap = saved_gate_up.shape[3]
    hid = down_weight.shape[1]
    split = hid - WAVE_TILES * TILE
    inner, outer = lax.axis_index("inner"), lax.axis_index("outer")
    z, y, x, core = inner // 4, inner % 4, outer // 2, outer % 2
    steps = jnp.array([0, -1, 1, 2], jnp.int32)

    gathered = lax.all_gather(down_weight[:, :split], "inner", axis=0, tiled=False)

    a, b = down_weight[0, split:], down_weight[1, split:]
    one = [along(a, "y", 1), along(a, "y", -1), along(b, "z", 1), along(b, "z", -1)]
    one, (next_one, mine) = together(one, [along_x(grad_out), grad_out])
    cut = a.shape[0] // 2
    two = [
        along(one[0][:cut], "y", 1), along(one[1][cut:], "y", -1),
        along(one[2][:cut], "z", 1), along(one[3][cut:], "z", -1),
    ]
    two, (next_two, last_one, named, scales) = together(
        two, [along_x(next_one), along_x(mine, -1), routes.T, route_weights.T]
    )
    block_a = jnp.stack([a, one[0], one[1], jnp.concatenate(two[:2])])
    block_b = jnp.stack([b, one[2], one[3], jnp.concatenate(two[2:])])
    three = [
        along(block_a, "z", 1), along(block_a, "z", -1), along(block_b, "y", 1), along(block_b, "y", -1)
    ]

    near = jnp.stack([grad_out, next_one, next_two])
    last_one = last_one[None]
    near_other, last_other = other_core(near), other_core(last_one)
    plans = lax.all_to_all(
        plan(named, scales, n_outer), "outer", split_axis=0, concat_axis=0, tiled=True
    )
    back = 2 * core - 1
    source = jnp.stack(
        [((x + n * back) % 4) * 2 + core for n in range(4)]
        + [((x - n * back) % 4) * 2 + 1 - core for n in range(4)]
    )
    filled = fill(source, [near, last_one, near_other, last_other], plans, cap)
    rows = filled[0].reshape(2, n_outer * cap, grad_out.shape[1])
    weights = filled[1].reshape(2, n_outer * cap, 128)
    out, sums = whole(rows, gathered, saved_gate_up, weights)

    three, (out, sums) = together(three, [out, sums])
    parts = halves(three)
    four = [
        along(parts[0], "z", 1), along(parts[1], "z", -1),
        along(parts[2], "y", 1), along(parts[3], "y", -1),
    ]
    (four,) = together(four)

    near_z, near_y = (z + steps) % 4, (y + steps) % 4
    order = jnp.concatenate(
        [
            (near_z[:, None] * 4 + near_y[None, :]).reshape(-1),
            (near_y[:, None] + near_z[None, :] * 4).reshape(-1),
        ]
    )
    partial = most(order, rows, [block_a, three[0], three[1], block_b, three[2], three[3]])
    out, grads = last(order, rows, four, saved_gate_up, weights, partial, sums, plans, out)
    returned = lax.all_to_all(grads, "outer", split_axis=0, concat_axis=0, tiled=True)
    return (out, pick(routes.T, returned).T)


def solution(mesh):
    in_specs = (
        P(("outer", "inner"), None),
        P(("outer", "inner"), None),
        P(("outer", "inner"), None),
        P(None, "outer", "inner", None, None),
        P("outer", None, "inner"),
    )
    out_specs = (P(None, "outer", "inner", None, None), P(("outer", "inner"), None))
    return jax.shard_map(shards, mesh=mesh, in_specs=in_specs, out_specs=out_specs, check_vma=False)
```
